256 devices in a mesh: sec: 4 (over x), gx: 8 (over z_lo, y), gy: 8 (over z_hi, core).
Axes of the slice: x: 4, y: 4, z: 8 (z_hi: 4, z_lo: 2; z = z_hi * 2 + z_lo), core: 2. Of those that a mesh axis runs over, the one named last changes fastest.
Arguments:
- air_surface: float32 [5, 256, 32, 4, 128], P(None, 'gx', 'gy', 'sec'), may hold values from -4 to 4
- remap_weights: bfloat16 [256, 32, 4, 2, 128, 128], P('gx', 'gy', 'sec'), may hold values from -0.25 to 0.25
- sources: int32 [256, 32, 4, 2], P('gx', 'gy', 'sec'), may hold values from 0 to 8
- live_count: int32 [256, 32, 4], P('gx', 'gy', 'sec'), may hold values from 1 to 2, as said below
- land_sea: int32 [256, 32], P('gx', 'gy'), may hold values from 0 to 1, as said below
- tracers: float32 [2, 40, 256, 4096], P(None, 'sec', 'gx', 'gy'), may hold values from -5 to 5
- currents: float32 [2, 40, 256, 4096], P(None, 'sec', 'gx', 'gy'), may hold values from -2 to 2
Outputs:
- tracers_out: float32 [2, 40, 256, 4096], P(None, 'sec', 'gx', 'gy')
- ocean_flux: float32 [4, 256, 4096], P(None, 'gx', 'gy')
The draws below stay inside these ranges and needn't reach their ends.
Inputs may be any that keep to these rules, and one draw needn't show every extreme that they name: `sources`: code c names the tile at offset (c // 3 - 1, c % 3 - 1) in ocean tiles from the destination, of the same quadrant as the slot. `live_count`: some tile and quadrant uses all 2 slots. `land_sea`: for every even column x >= 2 some tile row has ocean at x and land at x - 1.
All inputs are finite; a program needn't handle non-finite values.
Results may differ from the reference program's by a relative error of at most 0.003.
Values may be sent and summed in bfloat16 or wider, within the bound.
No kernel may reach another device: no remote copies, remote signals or barrier semaphores. Data moves between devices by JAX's collectives and lax.ppermute only.
A program may use at most 128 MiB of HBM per device.

```python
import jax
import jax.numpy as jnp
from jax import lax

TILE = 128
SLOTS = 2
STEPS = 3
QUADS = 4
NX = 256
NTY = 32
NY = 4096
NLEV = 40


def draw_live_count(key, part):
    key = jax.random.fold_in(key, 7)
    count_key, spot_key = jax.random.split(key)
    counts = jax.random.randint(count_key, (NX * NTY * QUADS,), 1, SLOTS + 1)
    position = jax.random.randint(spot_key, (), 0, NX * NTY * QUADS)
    counts = counts.at[position].set(SLOTS)
    return counts.reshape(NX, NTY, QUADS).astype(jnp.int32)


def draw_land_sea(key, part):
    key = jax.random.fold_in(key, 11)
    base_key, row_key = jax.random.split(key)
    base = jax.random.randint(base_key, (NX, NTY), 0, 4)
    base = jnp.where(base < 3, 1, 0).astype(jnp.int32)
    chosen = jax.random.randint(row_key, (NX,), 0, NTY).astype(jnp.int32)
    column_ids = jnp.arange(NX, dtype=jnp.int32)
    row_ids = jnp.arange(NTY, dtype=jnp.int32)
    even_edge = (column_ids % 2 == 0) & (column_ids >= 2)
    set_sea = even_edge[:, None] & (row_ids[None, :] == chosen[:, None])
    next_even = jnp.concatenate([even_edge[1:], jnp.zeros((1,), dtype=bool)])
    next_chosen = jnp.concatenate([chosen[1:], jnp.zeros((1,), dtype=jnp.int32)])
    set_land = next_even[:, None] & (row_ids[None, :] == next_chosen[:, None])
    result = jnp.where(set_sea, 1, base)
    result = jnp.where(set_land, 0, result)
    return result.astype(jnp.int32)


def touch_ends(entries, rng, low, top_value):
    index_at = [jax.random.randint(jax.random.fold_in(rng, axis), (), 0, length) for axis, length in enumerate(entries.shape)]
    main_axis = entries.shape.index(max(entries.shape))
    neighbour = index_at[:main_axis] + [(index_at[main_axis] + 1) % entries.shape[main_axis]] + index_at[main_axis + 1:]
    return entries.at[tuple(index_at)].set(low).at[tuple(neighbour)].set(top_value)


def steps_of(rng, dims, cuts, smallest, largest):
    loudness = 1.0
    for axis_at, shards_of in cuts:
        draws = jax.random.uniform(jax.random.fold_in(jax.random.fold_in(rng, 6), axis_at), (shards_of,), jnp.float32, smallest / len(cuts), largest / len(cuts))
        loudness = loudness * jnp.repeat(jnp.exp(draws), dims[axis_at] // shards_of).reshape((-1,) + (1,) * (len(dims) - 1 - axis_at))
    return loudness


def noise(stream_key, extent, deviation, limit, cuts=(), kind=jnp.bfloat16):
    gain = steps_of(stream_key, extent, cuts, -0.22, 0.18) if cuts else 1.0
    values = jax.random.normal(stream_key, extent, jnp.float32) * deviation * gain
    return jnp.minimum(jnp.maximum(values, -limit), limit).astype(kind)


def setup_inputs(seed: int = 0) -> dict:
    arg_keys = jax.random.split(jax.random.key(seed), 8)
    air_surface = noise(arg_keys[0], (5, NX, NTY, QUADS, TILE), 1.0, 4.0, ((1, 8), (2, 8), (3, 4)), jnp.float32)
    remap_weights = noise(arg_keys[1], (NX, NTY, QUADS, SLOTS, TILE, TILE), (2 * SLOTS * TILE) ** -0.5, 0.25, ((0, 8), (1, 8), (2, 4)))
    sources = touch_ends(jax.random.randint(arg_keys[2], (NX, NTY, QUADS, SLOTS), 0, 9), jax.random.fold_in(arg_keys[2], 1), 0, 8).astype(jnp.int32)
    live_count = draw_live_count(jax.random.fold_in(arg_keys[7], 71), 0)
    land_sea = draw_land_sea(jax.random.fold_in(arg_keys[7], 71), 0)
    tracers = noise(arg_keys[5], (2, NLEV, NX, NY), 1.0, 5.0, ((1, 4), (2, 8), (3, 8)), jnp.float32)
    currents = noise(arg_keys[6], (2, NLEV, NX, NY), 0.5, 2.0, ((1, 4), (2, 8), (3, 8)), jnp.float32)
    return {"air_surface": air_surface, "remap_weights": remap_weights, "sources": sources, "live_count": live_count, "land_sea": land_sea, "tracers": tracers, "currents": currents}


drag_coef = 0.6
wind_gain = 0.5
heat_gain = 0.5
salt_gain = 0.5
diffusion = 0.15
advection = 0.5
vertical_mix = 0.2

def bulk_fluxes(air_surface):
    wind_u = air_surface[0]
    wind_v = air_surface[1]
    air_temp = air_surface[2]
    humidity = air_surface[3]
    skin_temp = air_surface[4]
    bulk_rate = (1.0 + 0.5 * jnp.tanh(skin_temp - air_temp)) * jnp.sqrt(wind_u * wind_u + wind_v * wind_v + 1.0)
    stacked = jnp.stack([drag_coef * bulk_rate * wind_u, drag_coef * bulk_rate * wind_v, drag_coef * bulk_rate * (skin_temp - air_temp), drag_coef * bulk_rate * (jnp.exp(0.3 * skin_temp) - humidity)])
    return stacked.astype(jnp.bfloat16)

def openings(level_ids, total_levels):
    up_open = (level_ids > 0).astype(jnp.float32)[:, None, None]
    down_open = (level_ids < total_levels - 1).astype(jnp.float32)[:, None, None]
    return (up_open, down_open)

def stencil(padded, mask_pad, east_flow, north_flow, up_open, down_open):
    centre = padded[:, 1:-1, 1:-1, 1:-1]
    mask_mid = mask_pad[1:-1, 1:-1, 1:-1]
    east_cell = padded[:, 1:-1, 2:, 1:-1]
    west_cell = padded[:, 1:-1, :-2, 1:-1]
    north_cell = padded[:, 1:-1, 1:-1, 2:]
    south_cell = padded[:, 1:-1, 1:-1, :-2]
    above_cell = padded[:, :-2, 1:-1, 1:-1]
    below_cell = padded[:, 2:, 1:-1, 1:-1]
    mask_east = mask_pad[1:-1, 2:, 1:-1]
    mask_west = mask_pad[1:-1, :-2, 1:-1]
    mask_north = mask_pad[1:-1, 1:-1, 2:]
    mask_south = mask_pad[1:-1, 1:-1, :-2]
    spread = mask_east * (east_cell - centre) + mask_west * (west_cell - centre) + mask_north * (north_cell - centre) + mask_south * (south_cell - centre)
    carried = east_flow * (mask_east * east_cell - mask_west * west_cell) + north_flow * (mask_north * north_cell - mask_south * south_cell)
    mixed = up_open * (above_cell - centre) + down_open * (below_cell - centre)
    return centre + mask_mid * (diffusion * spread - advection * carried + vertical_mix * mixed)

def reference(air_surface, remap_weights, sources, live_count, land_sea, tracers, currents):
    fluxes = bulk_fluxes(air_surface)
    padded_flux = jnp.pad(fluxes, ((0, 0), (1, 1), (1, 1), (0, 0), (0, 0)))
    quadrant = jnp.arange(QUADS).astype(jnp.int32)[None, :, None]
    tile_rows = jnp.arange(NTY).astype(jnp.int32)[:, None, None]
    slot_ids = jnp.arange(SLOTS).astype(jnp.int32)

    def one_column(column):
        band_rows = lax.dynamic_slice_in_dim(padded_flux, column, 3, 1)
        source_code = lax.dynamic_index_in_dim(sources, column, 0, keepdims=False)
        live_slots = lax.dynamic_index_in_dim(live_count, column, 0, keepdims=False)
        weights = lax.dynamic_index_in_dim(remap_weights, column, 0, keepdims=False)
        blocks = band_rows[:, source_code // 3, tile_rows + source_code % 3, quadrant]
        live_mask = slot_ids[None, None, :] < live_slots[:, :, None]
        blocks = jnp.where(live_mask[None, :, :, :, None], blocks.astype(jnp.float32), 0.0)
        result = jnp.einsum('ftqsc,tqsdc->ftd', blocks, weights.astype(jnp.float32))
        return result.reshape(4, NY)
    remapped = lax.map(one_column, jnp.arange(NX).astype(jnp.int32))
    cell_mask = jnp.repeat(land_sea.astype(jnp.float32), TILE, axis=1)
    ocean_flux = jnp.transpose(remapped, (1, 0, 2)) * cell_mask
    level_zero = (jnp.arange(NLEV) == 0).astype(jnp.float32)[:, None, None]
    forced_u = currents[0] + wind_gain * level_zero * ocean_flux[0]
    forced_v = currents[1] + wind_gain * level_zero * ocean_flux[1]
    heated = tracers[0] + heat_gain * level_zero * ocean_flux[2]
    freshened = tracers[1] - salt_gain * level_zero * ocean_flux[3]
    fields = jnp.stack([heated, freshened])
    mask_pad = jnp.pad(jnp.broadcast_to(cell_mask, (NLEV, NX, NY)), 1)
    up_open, down_open = openings(jnp.arange(NLEV).astype(jnp.int32), NLEV)
    for step_index in range(STEPS):
        padded = jnp.pad(fields, ((0, 0), (1, 1), (1, 1), (1, 1)))
        fields = stencil(padded, mask_pad, forced_u, forced_v, up_open, down_open)
    return (fields, ocean_flux)
```

```python
import jax
import jax.numpy as jnp
from jax import lax
from jax.experimental import pallas as pl
from jax.experimental.pallas import tpu as pltpu
from jax.sharding import PartitionSpec as P

f32 = jnp.float32
bf16 = jnp.bfloat16

DRAG = 0.6
WIND_GAIN = 0.5
HEAT_GAIN = 0.5
SALT_GAIN = 0.5
DIFFUSION = 0.15
ADVECTION = 0.5
VERTICAL = 0.2

NX = 32
NT = 4
NL = 10
LANES = 128

YF, YW, YC, YT, YROWS = 0, 256, 448, 464, 528
XPLANE, XF, XROWS = 176, 880, 912
CZ, CROWS = 640, 1024

VMEM_BYTES = 48 * 1024 * 1024

PLANES = (
    [("t", 0, level) for level in range(NL)]
    + [("t", 1, level) for level in range(NL)]
    + [("c", 0, 0), ("c", 0, 9), ("c", 1, 0), ("c", 1, 9)]
    + [("c", 0, level) for level in range(1, 9)]
    + [("c", 1, level) for level in range(1, 9)]
)
MASK_PLANE = len(PLANES)
PLANE_AT = {plane: index for index, plane in enumerate(PLANES)}


def column(row):
    rows = lax.broadcasted_iota(jnp.int32, (NX, NX), 0)
    cols = lax.broadcasted_iota(jnp.int32, (NX, NX), 1)
    return jnp.sum(jnp.where(rows == cols, jnp.broadcast_to(row, (NX, NX)), 0.0), axis=1, keepdims=True)


def lane_ids(shape):
    return lax.broadcasted_iota(jnp.int32, shape, len(shape) - 1)


def slot_codes(src, live):
    slot = lax.broadcasted_iota(jnp.int32, (NT, 2, NX), 1)
    return jnp.where(slot < live[...], src[...], 9).astype(f32)


def roll(value, shift, axis):
    shift %= value.shape[axis]
    return value if shift == 0 else pltpu.roll(value, shift, axis)


def unpack_north(pack, plane, rows=slice(None)):
    return roll(pack[plane // 32][rows], -4 * (plane % 32), 1)


def unpack_south(pack, plane, rows=slice(None)):
    return roll(pack[plane // 32][rows], 4 * (plane % 32), 1)


def pack_y_kernel(air, src, live, land, w, tr, cu, yn, ys, flux, air_s, wn, ws, rows_s, code_s, edge, sems):
    copies = [pltpu.make_async_copy(air.at[:, :, t, 0, :], air_s.at[t], sems.at[t]) for t in range(NT)]
    copies.append(pltpu.make_async_copy(w.at[:, NT - 1, 0, :, pl.ds(112, 16), :], wn, sems.at[4]))
    copies.append(pltpu.make_async_copy(w.at[:, 0, 0, :, pl.ds(0, 16), :], ws, sems.at[5]))
    for k, source in enumerate((tr, cu)):
        copies.append(pltpu.make_async_copy(source.at[:, :, :, pl.ds(384, 128)], edge.at[0, k], sems.at[6 + k]))
        copies.append(pltpu.make_async_copy(source.at[:, :, :, pl.ds(0, 128)], edge.at[1, k], sems.at[8 + k]))
    for copy in copies:
        copy.start()
    codes = slot_codes(src, live)
    code_s[...] = jnp.zeros((16, LANES), f32)
    for t in range(NT):
        code_s[2 * t : 2 * t + 2, 0:NX] = codes[t]
    table = code_s[...].astype(bf16)
    yn[YC : YC + 16, :] = table
    ys[YC : YC + 16, :] = table
    for t in range(NT):
        copies[t].wait()
        u, v, ta, qa, ts = (air_s[t, k] for k in range(5))
        rate = DRAG * (1.0 + 0.5 * jnp.tanh(ts - ta)) * jnp.sqrt(u * u + v * v + 1.0)
        values = (rate * u, rate * v, rate * (ts - ta), rate * (jnp.exp(0.3 * ts) - qa))
        for f, value in enumerate(values):
            value = value.astype(bf16)
            flux[t, f] = value
            at = YF + ((t % 2) * 4 + f) * NX
            (ys if t < 2 else yn)[at : at + NX, :] = value
    for copy in copies[4:]:
        copy.wait()
    for send, tile, first in ((yn, wn, 13), (ys, ws, 0)):
        for x in range(NX):
            for s in range(2):
                block = tile[x, s].astype(f32)
                for d in range(3):
                    rows_s[pl.ds(d * 64 + s * 32 + x, 1), :] = block[first + d : first + d + 1]
        send[YW : YW + 192, :] = rows_s[...].astype(bf16)
    group = lane_ids((NX, LANES)) // 4
    for side, send in enumerate((yn, ys)):
        mask_tile = land[NT - 1 if side == 0 else 0 : NT if side == 0 else 1, :].astype(f32)
        for part in range(2):
            pack = jnp.zeros((NX, LANES), f32)
            for at in range(32):
                plane = part * 32 + at
                if plane > MASK_PLANE:
                    break
                if plane == MASK_PLANE:
                    value = jnp.broadcast_to(column(mask_tile), (NX, LANES))
                else:
                    kind, c, level = PLANES[plane]
                    value = edge[side, 0 if kind == "t" else 1, c, level]
                if side == 0:
                    pack = jnp.where(group == 31 - at, roll(value, -4 * at, 1), pack)
                else:
                    pack = jnp.where(group == at, roll(value, 4 * at, 1), pack)
            send[YT + part * NX : YT + (part + 1) * NX, :] = pack.astype(bf16)


def pack_z_kernel(tr, cu, zu, zd, t_s, c_s, sems):
    copies = [
        pltpu.make_async_copy(tr.at[:, pl.ds(0, 3)], t_s.at[0], sems.at[0]),
        pltpu.make_async_copy(cu.at[:, pl.ds(0, 2)], c_s.at[0], sems.at[1]),
        pltpu.make_async_copy(tr.at[:, pl.ds(NL - 3, 3)], t_s.at[1], sems.at[2]),
        pltpu.make_async_copy(cu.at[:, pl.ds(NL - 2, 2)], c_s.at[1], sems.at[3]),
    ]
    for copy in copies:
        copy.start()
    for copy in copies:
        copy.wait()
    for side, send in enumerate((zu, zd)):
        for c in range(2):
            for level in range(3):
                send[c * 3 + level] = t_s[side, c, level].astype(bf16)
            for level in range(2):
                send[6 + c * 2 + level] = c_s[side, c, level].astype(bf16)


def field_packs(y):
    return (y[YT : YT + NX, :].astype(f32), y[YT + NX : YT + 2 * NX, :].astype(f32))


def pack_x_kernel(flux, yn_r, ys_r, land, tr, cu, xe, xw, rows_s, edge, sems):
    copies = []
    for k, source in enumerate((tr, cu)):
        copies.append(pltpu.make_async_copy(source.at[:, :, pl.ds(0, 8), :], edge.at[0, k], sems.at[2 * k]))
        copies.append(pltpu.make_async_copy(source.at[:, :, pl.ds(24, 8), :], edge.at[1, k], sems.at[2 * k + 1]))
    for copy in copies:
        copy.start()
    south, north = field_packs(yn_r), field_packs(ys_r)
    low = lane_ids((8, LANES)) < 64
    masks = [column(land[t : t + 1, :].astype(f32)) for t in range(NT)]
    for copy in copies:
        copy.wait()
    for side, send in enumerate((xw, xe)):
        rows = slice(0, 8) if side == 0 else slice(24, 32)
        keep = slice(0, 4) if side == 0 else slice(4, 8)
        x = 0 if side == 0 else NX - 1
        rows_s[...] = jnp.zeros((XROWS, LANES), f32)
        for plane in range(MASK_PLANE + 1):
            edge_col = jnp.where(low, unpack_north(north, plane, rows), unpack_south(south, plane, rows))
            rows_s[4 * XPLANE + plane * 4 : 4 * XPLANE + plane * 4 + 4, :] = edge_col[keep]
            for c in range(4):
                if plane == MASK_PLANE:
                    value = jnp.broadcast_to(masks[c][rows], (8, LANES))
                else:
                    kind, component, level = PLANES[plane]
                    value = edge[side, 0 if kind == "t" else 1, component, level, :, c * LANES : (c + 1) * LANES]
                rows_s[c * XPLANE + plane * 4 : c * XPLANE + plane * 4 + 4, :] = value[keep]
        for t in range(8):
            for f in range(4):
                if 2 <= t < 6:
                    block = flux[t - 2, f].astype(f32)
                else:
                    got, half = (yn_r, t) if t < 2 else (ys_r, t - 6)
                    at = YF + (half * 4 + f) * NX
                    block = got[at : at + NX, :].astype(f32)
                rows_s[XF + t * 4 + f : XF + t * 4 + f + 1, :] = block[x : x + 1]
        send[...] = rows_s[...].astype(bf16)


def remap_kernel(flux, yn_r, ys_r, xe_r, xw_r, src, live, w, part, up, down, across, rim, rhs, wbuf, sems):
    copies = []
    for t in range(NT):
        for half in range(2):
            rows = pl.ds(half * 16, 16)
            copies.append(pltpu.make_async_copy(w.at[rows, t, 0], wbuf.at[t, rows], sems.at[2 * t + half]))
    for copy in copies:
        copy.start()

    west = xe_r[XF : XF + 32, :].astype(f32)
    east = xw_r[XF : XF + 32, :].astype(f32)
    for t in range(8):
        for f in range(4):
            if 2 <= t < 6:
                block = flux[t - 2, f]
            else:
                got, half = (yn_r, t) if t < 2 else (ys_r, t - 6)
                at = YF + (half * 4 + f) * NX
                block = got[at : at + NX, :]
            rim[t, f, 8 : 8 + NX, :] = block.astype(f32)
            rim[t, f, 7:8, :] = west[t * 4 + f : t * 4 + f + 1]
            rim[t, f, 8 + NX : 9 + NX, :] = east[t * 4 + f : t * 4 + f + 1]

    def blocks(tile, row):
        code = jnp.broadcast_to(column(row), (NX, LANES))
        picked = [code == float(k) for k in range(9)]
        result = []
        for f in range(4):
            block = jnp.zeros((NX, LANES), f32)
            for k in range(9):
                x0 = 7 + k // 3
                block = jnp.where(picked[k], rim[tile + 2 + k % 3 - 1, f, x0 : x0 + NX, :], block)
            result.append(block)
        return result

    codes = slot_codes(src, live)
    for t in range(NT):
        for s in range(2):
            stacked = jnp.concatenate(blocks(t, codes[t, s : s + 1, :]), axis=0)
            rhs[t, s * LANES : (s + 1) * LANES, :] = stacked.T.astype(bf16)

    lane = lane_ids((NX, LANES))
    edges = [jnp.zeros((NX, LANES), f32) for f in range(4)]
    for got, tile, row, at in ((yn_r, -1, 6, 125), (ys_r, NT, 0, 0)):
        table = got[YC : YC + 16, :].astype(f32)
        picked = [blocks(tile, table[row + s : row + s + 1, 0:NX]) for s in range(2)]
        for d in range(3):
            weight = [
                got[YW + (d * 2 + s) * NX : YW + (d * 2 + s + 1) * NX, :].astype(f32) for s in range(2)
            ]
            for f in range(4):
                total = jnp.sum(weight[0] * picked[0][f] + weight[1] * picked[1][f], axis=1, keepdims=True)
                edges[f] = jnp.where(lane == at + d, total, edges[f])
    for f in range(4):
        part[4 * LANES + f * NX : 4 * LANES + (f + 1) * NX, :] = edges[f]

    own = lane_ids((LANES, LANES)) % NX
    for t in range(NT):
        acc = jnp.zeros((LANES, LANES), f32)
        for half in range(2):
            copies[2 * t + half].wait()

            def one(x, acc, t=t):
                weights = jnp.concatenate([wbuf[t, x, 0], wbuf[t, x, 1]], axis=1)
                product = jnp.dot(weights, rhs[t], preferred_element_type=f32)
                return jnp.where(own == x, product, acc)

            acc = lax.fori_loop(half * 16, half * 16 + 16, one, acc, unroll=4)
        part[t * LANES : (t + 1) * LANES, :] = acc.T

    whole = part[...].astype(bf16)
    for send in (up, down, across):
        send[0:CZ, :] = whole
    for send, first in ((up, 0), (down, 32)):
        for side, got in enumerate((xw_r, xe_r)):
            for c in range(5):
                base = c * XPLANE
                if first == 0:
                    heat = got[base : base + 16, :].astype(f32)[0:8]
                    salt = got[base + 32 : base + 48, :].astype(f32)[8:16]
                else:
                    heat = got[base + 32 : base + 48, :].astype(f32)[0:8]
                    salt = got[base + 64 : base + 80, :].astype(f32)[8:16]
                at = CZ + (side * 5 + c) * 32
                send[at : at + 16, :] = jnp.concatenate([heat, salt], axis=0).astype(bf16)
                send[at + 16 : at + 32, :] = got[base + 80 : base + 96, :]
        send[CZ + 320 : CZ + 352, :] = yn_r[YT : YT + NX, :]
        send[CZ + 352 : CZ + 384, :] = ys_r[YT : YT + NX, :]


def flux_kernel(part, up_r, down_r, across_r, land, yn_r, ys_r, out, ext, de, dw, rows_s):
    south, north = field_packs(yn_r), field_packs(ys_r)
    low = lane_ids((NX, LANES)) < 64
    for c in range(5):
        if c < 4:
            mask = jnp.broadcast_to(column(land[c : c + 1, :].astype(f32)), (NX, LANES))
        else:
            mask = jnp.where(low, unpack_north(north, MASK_PLANE), unpack_south(south, MASK_PLANE))
        for f in range(4):
            at = c * LANES + f * NX
            total = part[at : at + NX, :] + up_r[at : at + NX, :].astype(f32)
            total = total + down_r[at : at + NX, :].astype(f32) + across_r[at : at + NX, :].astype(f32)
            total = total * mask
            if c < 4:
                out[f, :, c * LANES : (c + 1) * LANES] = total
            ext[f, c] = total
            rows_s[0, c * 16 + f * 4 : c * 16 + f * 4 + 4, :] = total[0:4]
            rows_s[1, c * 16 + f * 4 : c * 16 + f * 4 + 4, :] = total[NX - 4 : NX]
    dw[...] = rows_s[0].astype(bf16)
    de[...] = rows_s[1].astype(bf16)


def lane_next(value, lane):
    rolled = pltpu.roll(value, LANES - 1, 2)
    return jnp.where(lane == LANES - 1, jnp.concatenate([rolled[1:], rolled[:1]], axis=0), rolled)


def lane_prev(value, lane):
    rolled = pltpu.roll(value, 1, 2)
    return jnp.where(lane == 0, jnp.concatenate([rolled[-1:], rolled[:-1]], axis=0), rolled)


def ocean_kernel(
    tr, cu, zu_r, zd_r, yn_r, ys_r, xe_r, xw_r, up_r, down_r, ext, de_r, dw_r, land, out,
    g0, g1, vel, mask, coef, force, xs,
):
    sec = lax.axis_index("sec")
    own, west, east = slice(12, 44), slice(8, 12), slice(44, 48)
    south, north = field_packs(yn_r), field_packs(ys_r)
    low = lane_ids((NX, LANES)) < 64

    xs[0] = xw_r[0:XF, :].astype(f32)
    xs[1] = xe_r[0:XF, :].astype(f32)

    def edge_col(plane):
        return jnp.where(low, unpack_north(north, plane), unpack_south(south, plane))

    for c in range(4):
        mask[c, own, :] = jnp.broadcast_to(column(land[c : c + 1, :].astype(f32)), (NX, LANES))
    mask[4, own, :] = edge_col(MASK_PLANE)
    for c in range(5):
        at = c * XPLANE + MASK_PLANE * 4
        mask[c, east, :] = xs[0, at : at + 4, :]
        mask[c, west, :] = xs[1, at : at + 4, :]

    lane = lane_ids((5, 8, LANES))
    for r in range(8, 48, 8):
        rows, m = slice(r, r + 8), mask[:, r : r + 8, :]
        around = mask[:, r + 1 : r + 9, :] + mask[:, r - 1 : r + 7, :] + lane_next(m, lane) + lane_prev(m, lane)
        coef[:, rows, :] = m * (1.0 - DIFFUSION * around)

    def put(ref, where, plane_rows, scale=None):
        for c in range(5):
            for rows, value in plane_rows(c):
                ref[where + (c, rows)] = value * mask[c, rows, :]

    for plane, (kind, c, level) in enumerate(PLANES):
        source = tr if kind == "t" else cu

        def pieces(col, plane=plane, source=source, c=c, level=level):
            if col < 4:
                body = source[c, level, :, col * LANES : (col + 1) * LANES]
            else:
                body = edge_col(plane)
            at = col * XPLANE + plane * 4
            return ((own, body), (east, xs[0, at : at + 4, :]), (west, xs[1, at : at + 4, :]))

        if kind == "t":
            put(g0, (c, level + 3), pieces)
        else:
            put(vel, (c, level + 2), pieces)

    for got, z, below in ((up_r, zu_r, True), (down_r, zd_r, False)):
        z_south = (got[CZ + 320 : CZ + 352, :].astype(f32),)
        z_north = (got[CZ + 352 : CZ + 384, :].astype(f32),)
        halo = [[got[CZ + (s * 5 + c) * 32 : CZ + (s * 5 + c + 1) * 32, :].astype(f32) for c in range(5)] for s in (0, 1)]
        for c in range(2):
            for k in range(3):
                at = (13 + k) if below else k
                for col in range(4):
                    body = z[c * 3 + k, :, col * LANES : (col + 1) * LANES].astype(f32)
                    g0[c, at, col, own, :] = body * mask[col, own, :]
                step = k if below else k - 1
                if not 0 <= step < 2:
                    continue
                plane = PLANE_AT[("t", c, k if below else 7 + k)]
                col4 = jnp.where(low, unpack_north(z_north, plane), unpack_south(z_south, plane))
                g0[c, at, 4, own, :] = col4 * mask[4, own, :]
                for col in range(5):
                    r = c * 8 + step * 4
                    g0[c, at, col, east, :] = halo[0][col][r : r + 4] * mask[col, east, :]
                    g0[c, at, col, west, :] = halo[1][col][r : r + 4] * mask[col, west, :]
            for k in range(2):
                at = (12 + k) if below else k
                for col in range(4):
                    body = z[6 + c * 2 + k, :, col * LANES : (col + 1) * LANES].astype(f32)
                    vel[c, at, col, own, :] = body * mask[col, own, :]
                if k != (0 if below else 1):
                    continue
                plane = PLANE_AT[("c", c, 0 if below else 9)]
                col4 = jnp.where(low, unpack_north(z_north, plane), unpack_south(z_south, plane))
                vel[c, at, 4, own, :] = col4 * mask[4, own, :]
                for col in range(5):
                    r = 16 + c * 8 + (0 if below else 4)
                    vel[c, at, col, east, :] = halo[0][col][r : r + 4] * mask[col, east, :]
                    vel[c, at, col, west, :] = halo[1][col][r : r + 4] * mask[col, west, :]

    @pl.when(sec == 0)
    def _():
        dw_f, de_f = dw_r[...].astype(f32), de_r[...].astype(f32)
        for f, (ref, at, gain) in enumerate(
            ((vel, (0, 2), WIND_GAIN), (vel, (1, 2), WIND_GAIN), (g0, (0, 3), HEAT_GAIN), (g0, (1, 3), -SALT_GAIN))
        ):
            for c in range(5):
                r = c * 16 + f * 4
                for rows, value in ((own, ext[f, c]), (east, dw_f[r : r + 4]), (west, de_f[r : r + 4])):
                    ref[at + (c, rows)] += gain * value * mask[c, rows, :]

    first = sec * NL - 3
    total_levels = NL * lax.axis_size("sec")

    def level_step(src, l, rows):
        level = first + l
        up = jnp.where(level > 0, VERTICAL, 0.0).astype(f32)
        down = jnp.where(level < total_levels - 1, VERTICAL, 0.0).astype(f32)
        r = rows.start
        m = mask[:, rows, :]
        a = (ADVECTION) * vel[0, l - 1, :, rows, :]
        b = (ADVECTION) * vel[1, l - 1, :, rows, :]
        base = DIFFUSION * m
        centre = coef[:, rows, :] - (up + down) * m
        mu, md = up * m, down * m
        results = []
        for c in range(2):
            g = src[c, l, :, rows, :]
            new = centre * g
            new += (base - a) * src[c, l, :, r + 1 : r + 9, :] + (base + a) * src[c, l, :, r - 1 : r + 7, :]
            new += (base - b) * lane_next(g, lane) + (base + b) * lane_prev(g, lane)
            new += mu * src[c, l - 1, :, rows, :] + md * src[c, l + 1, :, rows, :]
            results.append(new)
        return results

    for step, (src, dst) in enumerate(((g0, g1), (g1, g0))):

        def one_level(l, _, src=src, dst=dst):
            for r in range(8, 48, 8):
                rows = slice(r, r + 8)
                for c, value in enumerate(level_step(src, l, rows)):
                    dst[c, l, :, rows, :] = value
            return 0

        lax.fori_loop(1 + step, 15 - step, one_level, 0)

    def last_level(l, _):
        for r in range(12, 44, 8):
            rows = slice(r, r + 8)
            for c, value in enumerate(level_step(g0, l, rows)):
                for col in range(4):
                    at = (c, l - 3, slice(r - 12, r - 4), slice(col * LANES, (col + 1) * LANES))
                    out[at] = jnp.where(mask[col, rows, :] > 0.0, value[col], tr[at])
        return 0

    lax.fori_loop(3, 13, last_level, 0)


ANY = pl.BlockSpec(memory_space=pl.ANY)
VMEM = pl.BlockSpec(memory_space=pltpu.VMEM)


def call(kernel, in_specs, outs, scratch, name, flops=0, bytes_accessed=0):
    return pl.pallas_call(
        kernel,
        out_shape=[jax.ShapeDtypeStruct(shape, dtype) for shape, dtype in outs],
        in_specs=in_specs,
        out_specs=[VMEM] * len(outs),
        scratch_shapes=scratch,
        compiler_params=pltpu.CompilerParams(vmem_limit_bytes=VMEM_BYTES),
        cost_estimate=pl.CostEstimate(flops=flops, bytes_accessed=bytes_accessed, transcendentals=0),
        name=name,
    )


def shifted(value, axis, step, wrap=False):
    count = lax.axis_size(axis)
    pairs = [(i, (i + step) % count) for i in range(count) if wrap or 0 <= i + step < count]
    return lax.ppermute(value, axis, pairs)


def on_device(air_surface, remap_weights, sources, live_count, land_sea, tracers, currents):
    src = jnp.transpose(sources[:, :, 0, :], (1, 2, 0))
    live = jnp.transpose(live_count, (1, 2, 0))
    land = jnp.transpose(land_sea, (1, 0))
    dma = pltpu.SemaphoreType.DMA

    yn, ys, flux = call(
        pack_y_kernel,
        [ANY, VMEM, VMEM, VMEM, ANY, ANY, ANY],
        [((YROWS, LANES), bf16), ((YROWS, LANES), bf16), ((NT, 4, NX, LANES), bf16)],
        [
            pltpu.VMEM((NT, 5, NX, LANES), f32),
            pltpu.VMEM((NX, 2, 16, LANES), bf16),
            pltpu.VMEM((NX, 2, 16, LANES), bf16),
            pltpu.VMEM((192, LANES), f32),
            pltpu.VMEM((16, LANES), f32),
            pltpu.VMEM((2, 2, 2, NL, NX, LANES), f32),
            dma((10,)),
        ],
        "pack_y",
        bytes_accessed=4_000_000,
    )(air_surface, src, live, land, remap_weights, tracers, currents)
    yn_r = shifted(yn, "gy", 1)
    ys_r = shifted(ys, "gy", -1)

    zu, zd = call(
        pack_z_kernel,
        [ANY, ANY],
        [((10, NX, 512), bf16)] * 2,
        [pltpu.VMEM((2, 2, 3, NX, 512), f32), pltpu.VMEM((2, 2, 2, NX, 512), f32), dma((4,))],
        "pack_z",
        bytes_accessed=4_000_000,
    )(tracers, currents)
    zu_r = shifted(zu, "sec", -1)
    zd_r = shifted(zd, "sec", 1)

    xe, xw = call(
        pack_x_kernel,
        [VMEM, VMEM, VMEM, VMEM, ANY, ANY],
        [((XROWS, LANES), bf16)] * 2,
        [pltpu.VMEM((XROWS, LANES), f32), pltpu.VMEM((2, 2, 2, NL, 8, 512), f32), dma((4,))],
        "pack_x",
        bytes_accessed=4_000_000,
    )(flux, yn_r, ys_r, land, tracers, currents)
    xe_r = shifted(xe, "gx", 1)
    xw_r = shifted(xw, "gx", -1)

    part, up, down, across = call(
        remap_kernel,
        [VMEM] * 7 + [ANY],
        [((CZ, LANES), f32), ((CROWS, LANES), bf16), ((CROWS, LANES), bf16), ((CZ, LANES), bf16)],
        [
            pltpu.VMEM((8, 4, 48, LANES), f32),
            pltpu.VMEM((NT, 2 * LANES, LANES), bf16),
            pltpu.VMEM((NT, NX, 2, LANES, LANES), bf16),
            dma((8,)),
        ],
        "remap",
        bytes_accessed=16_000_000,
    )(flux, yn_r, ys_r, xe_r, xw_r, src, live, remap_weights)
    up_r = shifted(up, "sec", -1, True)
    down_r = shifted(down, "sec", 1, True)
    across_r = shifted(across, "sec", 2, True)

    ocean_flux, ext, de, dw = call(
        flux_kernel,
        [VMEM] * 7,
        [((4, NX, 512), f32), ((4, 5, NX, LANES), f32), ((80, LANES), bf16), ((80, LANES), bf16)],
        [pltpu.VMEM((2, 80, LANES), f32)],
        "flux_sum",
        bytes_accessed=4_000_000,
    )(part, up_r, down_r, across_r, land, yn_r, ys_r)
    de_r = shifted(de, "gx", 1)
    dw_r = shifted(dw, "gx", -1)

    (tracers_out,) = call(
        ocean_kernel,
        [VMEM] * 14,
        [((2, NL, NX, 512), f32)],
        [
            pltpu.VMEM((2, 16, 5, 56, LANES), f32),
            pltpu.VMEM((2, 16, 5, 56, LANES), f32),
            pltpu.VMEM((2, 14, 5, 56, LANES), f32),
            pltpu.VMEM((5, 56, LANES), f32),
            pltpu.VMEM((5, 56, LANES), f32),
            pltpu.VMEM((4, 5, 56, LANES), f32),
            pltpu.VMEM((2, XF, LANES), f32),
        ],
        "ocean",
        bytes_accessed=16_000_000,
    )(tracers, currents, zu_r, zd_r, yn_r, ys_r, xe_r, xw_r, up_r, down_r, ext, de_r, dw_r, land)
    return (tracers_out, ocean_flux)


def solution(mesh):
    return jax.shard_map(
        on_device,
        mesh=mesh,
        in_specs=(
            P(None, "gx", "gy", "sec", None),
            P("gx", "gy", "sec", None, None, None),
            P("gx", "gy", "sec", None),
            P("gx", "gy", "sec"),
            P("gx", "gy"),
            P(None, "sec", "gx", "gy"),
            P(None, "sec", "gx", "gy"),
        ),
        out_specs=(P(None, "sec", "gx", "gy"), P(None, "gx", "gy")),
        check_vma=False,
    )
```

```python
import jax
import jax.numpy as jnp
from jax import lax
from jax.experimental import pallas as pl
from jax.experimental.pallas import tpu as pltpu
from jax.sharding import PartitionSpec as P

f32 = jnp.float32
bf16 = jnp.bfloat16

DRAG = 0.6
WIND_GAIN = 0.5
HEAT_GAIN = 0.5
SALT_GAIN = 0.5
DIFFUSION = 0.15
ADVECTION = 0.5
VERTICAL = 0.2

NX = 32
NT = 4
NL = 10
LANES = 128

YF, YW, YC, YT, YROWS = 0, 256, 448, 464, 528
XPLANE, XF, XROWS = 176, 880, 912
CROWS = 528
ZROWS = 384
LAND = 8

VMEM_BYTES = 24 * 1024 * 1024

PLANES = (
    [("t", 0, level) for level in range(NL)]
    + [("t", 1, level) for level in range(NL)]
    + [("c", 0, 0), ("c", 0, 9), ("c", 1, 0), ("c", 1, 9)]
    + [("c", 0, level) for level in range(1, 9)]
    + [("c", 1, level) for level in range(1, 9)]
)
MASK_PLANE = len(PLANES)
PLANE_AT = {plane: index for index, plane in enumerate(PLANES)}


def column(row):
    rows = lax.broadcasted_iota(jnp.int32, (NX, NX), 0)
    cols = lax.broadcasted_iota(jnp.int32, (NX, NX), 1)
    return jnp.sum(jnp.where(rows == cols, jnp.broadcast_to(row, (NX, NX)), 0.0), axis=1, keepdims=True)


def lane_ids(shape):
    return lax.broadcasted_iota(jnp.int32, shape, len(shape) - 1)


def start(*copies):
    for copy in copies:
        copy.start()


def wait(*copies):
    for copy in copies:
        copy.wait()


def roll(value, shift, axis):
    shift %= value.shape[axis]
    return value if shift == 0 else pltpu.roll(value, shift, axis)


def unpack_north(pack, plane, rows=slice(None)):
    return roll(pack[plane // 32][rows], -4 * (plane % 32), 1)


def unpack_south(pack, plane, rows=slice(None)):
    return roll(pack[plane // 32][rows], 4 * (plane % 32), 1)


def pack_y_kernel(
    air, src_h, live_h, land_h, w, tr, cu, yn, ys, flux, table, src, live, land, air_s, wn, ws, rows_s, edge, sems
):
    copies = [pltpu.make_async_copy(air.at[:, :, t, 0, :], air_s.at[t], sems.at[t]) for t in range(NT)]
    copies.append(pltpu.make_async_copy(w.at[:, NT - 1, 0, :, pl.ds(112, 16), :], wn, sems.at[4]))
    copies.append(pltpu.make_async_copy(w.at[:, 0, 0, :, pl.ds(0, 16), :], ws, sems.at[5]))
    for k, source in enumerate((tr, cu)):
        copies.append(pltpu.make_async_copy(source.at[:, :, :, pl.ds(384, 128)], edge.at[0, k], sems.at[6 + k]))
        copies.append(pltpu.make_async_copy(source.at[:, :, :, pl.ds(0, 128)], edge.at[1, k], sems.at[8 + k]))
    small = [
        pltpu.make_async_copy(source, target, sems.at[10 + k])
        for k, (source, target) in enumerate(((src_h, src), (live_h, live), (land_h, land)))
    ]
    start(*copies[:4], *small, *copies[4:])
    for t in range(NT):
        copies[t].wait()
        u, v, ta, qa, ts = (air_s[t, k] for k in range(5))
        rate = DRAG * (1.0 + 0.5 * jnp.tanh(ts - ta)) * jnp.sqrt(u * u + v * v + 1.0)
        values = (rate * u, rate * v, rate * (ts - ta), rate * (jnp.exp(0.3 * ts) - qa))
        for f, value in enumerate(values):
            value = value.astype(bf16)
            flux[t, f] = value
            at = YF + ((t % 2) * 4 + f) * NX
            (ys if t < 2 else yn)[at : at + NX, :] = value
    wait(*small)
    slot = lax.broadcasted_iota(jnp.int32, (NT, 2, NX), 1)
    codes = jnp.where(slot < live[...], src[...], 9).astype(f32)
    table[...] = jnp.zeros((16, LANES), f32)
    for t in range(NT):
        table[2 * t : 2 * t + 2, 0:NX] = codes[t]
    table[LAND : LAND + NT, 0:NX] = land[...].astype(f32)
    sent = table[...].astype(bf16)
    yn[YC : YC + 16, :] = sent
    ys[YC : YC + 16, :] = sent
    wait(*copies[4:])
    for send, tile, first in ((yn, wn, 13), (ys, ws, 0)):
        for x in range(NX):
            for s in range(2):
                block = tile[x, s].astype(f32)
                for d in range(3):
                    rows_s[pl.ds(d * 64 + s * 32 + x, 1), :] = block[first + d : first + d + 1]
        send[YW : YW + 192, :] = rows_s[...].astype(bf16)
    group = lane_ids((NX, LANES)) // 4
    for side, send in enumerate((yn, ys)):
        mask_tile = land[NT - 1 if side == 0 else 0 : NT if side == 0 else 1, :].astype(f32)
        for part in range(2):
            pack = jnp.zeros((NX, LANES), f32)
            for at in range(32):
                plane = part * 32 + at
                if plane > MASK_PLANE:
                    break
                if plane == MASK_PLANE:
                    value = jnp.broadcast_to(column(mask_tile), (NX, LANES))
                else:
                    kind, c, level = PLANES[plane]
                    value = edge[side, 0 if kind == "t" else 1, c, level]
                if side == 0:
                    pack = jnp.where(group == 31 - at, roll(value, -4 * at, 1), pack)
                else:
                    pack = jnp.where(group == at, roll(value, 4 * at, 1), pack)
            send[YT + part * NX : YT + (part + 1) * NX, :] = pack.astype(bf16)


def pack_z_kernel(tr, cu, after, zu, zd, t_s, c_s, sems):
    copies = [
        pltpu.make_async_copy(tr.at[:, pl.ds(0, 3)], t_s.at[0], sems.at[0]),
        pltpu.make_async_copy(cu.at[:, pl.ds(0, 2)], c_s.at[0], sems.at[1]),
        pltpu.make_async_copy(tr.at[:, pl.ds(NL - 3, 3)], t_s.at[1], sems.at[2]),
        pltpu.make_async_copy(cu.at[:, pl.ds(NL - 2, 2)], c_s.at[1], sems.at[3]),
    ]
    for copy in copies:
        copy.start()
    for copy in copies:
        copy.wait()
    for side, send in enumerate((zu, zd)):
        for c in range(2):
            for level in range(3):
                send[c * 3 + level] = t_s[side, c, level].astype(bf16)
            for level in range(2):
                send[6 + c * 2 + level] = c_s[side, c, level].astype(bf16)


def inside(axis, low):
    at = lax.axis_index(axis)
    return jnp.where(at > 0 if low else at < lax.axis_size(axis) - 1, 1.0, 0.0).astype(f32)


def field_packs(y):
    return (y[YT : YT + NX, :].astype(f32), y[YT + NX : YT + 2 * NX, :].astype(f32))


def pack_x_kernel(flux, yn_r, ys_r, table, tr, cu, xe, xw, rows_s, edge, sems):
    copies = []
    for k, source in enumerate((tr, cu)):
        copies.append(pltpu.make_async_copy(source.at[:, :, pl.ds(0, 8), :], edge.at[0, k], sems.at[2 * k]))
        copies.append(pltpu.make_async_copy(source.at[:, :, pl.ds(24, 8), :], edge.at[1, k], sems.at[2 * k + 1]))
    for copy in copies:
        copy.start()
    south, north = field_packs(yn_r), field_packs(ys_r)
    low = lane_ids((8, LANES)) < 64
    masks = [column(table[LAND + t : LAND + t + 1, 0:NX]) for t in range(NT)]
    in_south, in_north = inside("gy", True), inside("gy", False)
    for copy in copies:
        copy.wait()
    for side, send in enumerate((xw, xe)):
        rows = slice(0, 8) if side == 0 else slice(24, 32)
        keep = slice(0, 4) if side == 0 else slice(4, 8)
        x = 0 if side == 0 else NX - 1
        rows_s[...] = jnp.zeros((XROWS, LANES), f32)
        for plane in range(MASK_PLANE + 1):
            edge_col = jnp.where(low, unpack_north(north, plane, rows), unpack_south(south, plane, rows))
            if plane == MASK_PLANE:
                edge_col = edge_col * jnp.where(low, in_north, in_south)
            rows_s[4 * XPLANE + plane * 4 : 4 * XPLANE + plane * 4 + 4, :] = edge_col[keep]
            for c in range(4):
                if plane == MASK_PLANE:
                    value = jnp.broadcast_to(masks[c][rows], (8, LANES))
                else:
                    kind, component, level = PLANES[plane]
                    value = edge[side, 0 if kind == "t" else 1, component, level, :, c * LANES : (c + 1) * LANES]
                rows_s[c * XPLANE + plane * 4 : c * XPLANE + plane * 4 + 4, :] = value[keep]
        for t in range(8):
            for f in range(4):
                if 2 <= t < 6:
                    block = flux[t - 2, f].astype(f32)
                else:
                    got, half = (yn_r, t) if t < 2 else (ys_r, t - 6)
                    at = YF + (half * 4 + f) * NX
                    block = got[at : at + NX, :].astype(f32) * (in_south if t < 2 else in_north)
                rows_s[XF + t * 4 + f : XF + t * 4 + f + 1, :] = block[x : x + 1]
        send[...] = rows_s[...].astype(bf16)


def remap_kernel(flux, yn_r, ys_r, table, w, after_x, part, wedge, rim, blk, wbuf, sems):
    copies = []
    for t in range(NT):
        for half in range(2):
            rows = pl.ds(half * 16, 16)
            copies.append(pltpu.make_async_copy(w.at[rows, t, 0], wbuf.at[t, rows], sems.at[2 * t + half]))
    start(*copies)

    zero = jnp.zeros((8, LANES), f32)
    in_south, in_north = inside("gy", True), inside("gy", False)
    for t in range(8):
        for f in range(4):
            if 2 <= t < 6:
                block = flux[t - 2, f].astype(f32)
            else:
                got, half = (yn_r, t) if t < 2 else (ys_r, t - 6)
                at = YF + (half * 4 + f) * NX
                block = got[at : at + NX, :].astype(f32) * (in_south if t < 2 else in_north)
            rim[t, f, 0:8, :] = zero
            rim[t, f, 8 : 8 + NX, :] = block
            rim[t, f, 8 + NX : 16 + NX, :] = zero

    def blocks(tile, row):
        code = jnp.broadcast_to(column(row), (NX, LANES))
        picked = [code == float(k) for k in range(9)]
        result = []
        for f in range(4):
            block = jnp.zeros((NX, LANES), f32)
            for k in range(9):
                x0 = 7 + k // 3
                block = jnp.where(picked[k], rim[tile + 2 + k % 3 - 1, f, x0 : x0 + NX, :], block)
            result.append(block)
        return result

    for t in range(NT):
        for s in range(2):
            row = 2 * t + s
            for f, block in enumerate(blocks(t, table[row : row + 1, 0:NX])):
                blk[row, f * NX : (f + 1) * NX, :] = block

    lane = lane_ids((NX, LANES))
    edges = [jnp.zeros((NX, LANES), f32) for f in range(4)]
    for got, tile, row, at in ((yn_r, -1, 6, 125), (ys_r, NT, 0, 0)):
        codes = got[YC : YC + 16, :].astype(f32)
        picked = [blocks(tile, codes[row + s : row + s + 1, 0:NX]) for s in range(2)]
        for d in range(3):
            weight = [
                got[YW + (d * 2 + s) * NX : YW + (d * 2 + s + 1) * NX, :].astype(f32) for s in range(2)
            ]
            for f in range(4):
                total = jnp.sum(weight[0] * picked[0][f] + weight[1] * picked[1][f], axis=1, keepdims=True)
                edges[f] = jnp.where(lane == at + d, total, edges[f])
    for f in range(4):
        part[4 * LANES + f * NX : 4 * LANES + (f + 1) * NX, :] = edges[f]

    for t in range(NT):
        for half in range(2):
            copies[2 * t + half].wait()

            def pair(i, _, t=t):
                x = 2 * i
                rows = [
                    jnp.concatenate([blk[2 * t + s, pl.ds(x + j, 8, stride=NX), :] for j in range(2)], axis=0)
                    for s in range(2)
                ]
                weights = jnp.concatenate(
                    [jnp.concatenate([wbuf[t, x + j, s] for s in range(2)], axis=1) for j in range(2)], axis=0
                )
                product = lax.dot_general(
                    jnp.concatenate(rows, axis=1).astype(bf16),
                    weights,
                    (((1,), (1,)), ((), ())),
                    preferred_element_type=f32,
                )
                for j in range(2):
                    block = product[8 * j : 8 * j + 4, j * LANES : (j + 1) * LANES]
                    part[pl.ds(t * LANES + x + j, 4, stride=NX), :] = block
                return 0

            lax.fori_loop(half * 8, half * 8 + 8, pair, 0, unroll=8)
        for side, x in enumerate((0, NX - 1)):
            for s in range(2):
                wedge[side, t, s] = wbuf[t, x, s]


def rim_kernel(first_part, wedge, yn_r, ys_r, xe_r, xw_r, table, part, send, z2u, z2d):
    part[...] = first_part[...]
    near = [got[XF : XF + 32, :].astype(f32) * inside("gx", side == 0) for side, got in enumerate((xe_r, xw_r))]

    def blocks(side, tile, codes, row):
        x = 0 if side == 0 else NX - 1
        code = jnp.broadcast_to(codes[row : row + 1, x : x + 1], (4, LANES))
        block = jnp.zeros((4, LANES), f32)
        for k in range(3):
            at = (tile + 1 + k) * 4
            block = jnp.where(code == float(6 * side + k), near[side][at : at + 4], block)
        return block

    own_codes = table[...]
    gap = jnp.zeros((4, LANES), f32)
    for t in range(NT):
        rows = [
            jnp.concatenate([blocks(0, t, own_codes, 2 * t + s), gap, blocks(1, t, own_codes, 2 * t + s), gap], axis=0)
            for s in range(2)
        ]
        weights = jnp.concatenate(
            [jnp.concatenate([wedge[side, t, s] for s in range(2)], axis=1) for side in range(2)], axis=0
        )
        product = lax.dot_general(
            jnp.concatenate(rows, axis=1).astype(bf16), weights, (((1,), (1,)), ((), ())), preferred_element_type=f32
        )
        for side, x in enumerate((0, NX - 1)):
            part[pl.ds(t * LANES + x, 4, stride=NX), :] += product[8 * side : 8 * side + 4, side * LANES : (side + 1) * LANES]
    lane = lane_ids((4, LANES))
    for side, x in enumerate((0, NX - 1)):
        added = jnp.zeros((4, LANES), f32)
        for got, tile, row, at in ((yn_r, -1, 6, 125), (ys_r, NT, 0, 0)):
            codes = got[YC : YC + 16, :].astype(f32)
            picked = [blocks(side, tile, codes, row + s) for s in range(2)]
            for d in range(3):
                total = jnp.zeros((4, LANES), f32)
                for s in range(2):
                    first = YW + (d * 2 + s) * NX
                    weight = got[first : first + NX, :].astype(f32)[x : x + 1]
                    total += weight * picked[s]
                added = jnp.where(lane == at + d, jnp.sum(total, axis=1, keepdims=True), added)
        part[pl.ds(4 * LANES + x, 4, stride=NX), :] += added

    send[0 : 4 * LANES, :] = part[0 : 4 * LANES, :].astype(bf16)
    turned = part[4 * LANES : 5 * LANES, :].T
    send[4 * LANES : CROWS, :] = jnp.concatenate([turned[0:8], turned[LANES - 8 :]], axis=0).astype(bf16)
    for target, first in ((z2u, 0), (z2d, 32)):
        for side, got in enumerate((xw_r, xe_r)):
            for c in range(5):
                base = c * XPLANE
                if first == 0:
                    heat = got[base : base + 16, :].astype(f32)[0:8]
                    salt = got[base + 32 : base + 48, :].astype(f32)[8:16]
                else:
                    heat = got[base + 32 : base + 48, :].astype(f32)[0:8]
                    salt = got[base + 64 : base + 80, :].astype(f32)[8:16]
                at = (side * 5 + c) * 32
                target[at : at + 16, :] = jnp.concatenate([heat, salt], axis=0).astype(bf16)
                target[at + 16 : at + 32, :] = got[base + 80 : base + 96, :]
        target[320:352, :] = yn_r[YT : YT + NX, :]
        target[352:384, :] = ys_r[YT : YT + NX, :]


def flux_kernel(part, up_r, down_r, across_r, mask, ext, de, dw, rows_s):
    got = [ref[4 * LANES : CROWS, :].astype(f32) for ref in (up_r, down_r, across_r)]
    turned = got[0] + got[1] + got[2]
    halo = jnp.concatenate([turned[0:8], jnp.zeros((LANES - 16, LANES), f32), turned[8:16]], axis=0).T
    for c in range(5):
        for f in range(4):
            at = c * LANES + f * NX
            total = part[at : at + NX, :]
            if c < 4:
                for ref in (up_r, down_r, across_r):
                    total = total + ref[at : at + NX, :].astype(f32)
            else:
                total = total + halo[f * NX : (f + 1) * NX]
            total = total * mask[c, OWN, :]
            ext[f, :, c * LANES : (c + 1) * LANES] = total
            rows_s[0, c * 16 + f * 4 : c * 16 + f * 4 + 4, :] = total[0:4]
            rows_s[1, c * 16 + f * 4 : c * 16 + f * 4 + 4, :] = total[NX - 4 : NX]
    dw[...] = rows_s[0].astype(bf16)
    de[...] = rows_s[1].astype(bf16)


def lane_next(value, lane):
    rolled = pltpu.roll(value, LANES - 1, 2)
    return jnp.where(lane == LANES - 1, jnp.concatenate([rolled[1:], rolled[:1]], axis=0), rolled)


def lane_prev(value, lane):
    rolled = pltpu.roll(value, 1, 2)
    return jnp.where(lane == 0, jnp.concatenate([rolled[-1:], rolled[:-1]], axis=0), rolled)


OWN, WEST, EAST = slice(12, 44), slice(8, 12), slice(44, 48)
PLANE = (5, 56, LANES)


def advance(src, at, vel, v, mask, coef, l, rows):
    level = lax.axis_index("sec") * NL + l - 3
    up = jnp.where(level > 0, VERTICAL, 0.0).astype(f32)
    down = jnp.where(level < NL * lax.axis_size("sec") - 1, VERTICAL, 0.0).astype(f32)
    r = rows.start
    lane = lane_ids((5, 8, LANES))
    m = mask[:, rows, :]
    a = ADVECTION * vel[0, v, :, rows, :]
    b = ADVECTION * vel[1, v, :, rows, :]
    base = DIFFUSION * m
    centre = coef[:, rows, :] - (up + down) * m
    mu, md = up * m, down * m
    results = []
    for c in range(2):
        g = src[c, at, :, rows, :]
        new = centre * g
        new += (base - a) * src[c, at, :, r + 1 : r + 9, :] + (base + a) * src[c, at, :, r - 1 : r + 7, :]
        new += (base - b) * lane_next(g, lane) + (base + b) * lane_prev(g, lane)
        new += mu * src[c, at - 1, :, rows, :] + md * src[c, at + 1, :, rows, :]
        results.append(new)
    return results


def sweep(src, dst, vel, mask, coef, levels, src_at, dst_at, vel_at):
    def one_level(l, _):
        for r in range(8, 48, 8):
            rows = slice(r, r + 8)
            for c, value in enumerate(advance(src, l - src_at, vel, l - vel_at, mask, coef, l, rows)):
                dst[c, l - dst_at, :, rows, :] = value
        return 0

    lax.fori_loop(levels[0], levels[1], one_level, 0)


def finish(src, out, vel, mask, coef, levels, src_at, out_at, vel_at, before, before_at):
    def one_level(l, _):
        for r in range(12, 44, 8):
            rows = slice(r, r + 8)
            for c, value in enumerate(advance(src, l - src_at, vel, l - vel_at, mask, coef, l, rows)):
                for col in range(4):
                    at = (slice(r - 12, r - 4), slice(col * LANES, (col + 1) * LANES))
                    kept = before[(c, l - before_at) + at]
                    out[(c, l - out_at) + at] = jnp.where(mask[col, rows, :] > 0.0, value[col], kept)
        return 0

    lax.fori_loop(levels[0], levels[1], one_level, 0)


def middle_kernel(
    tr_h, cu_h, yn_r, ys_r, xe_r, xw_r, table, after, after_zu, after_zd, g0, vel, g1, g2, mask, coef, done, tr, cu, xs, sems
):
    copies = [pltpu.make_async_copy(tr_h, tr, sems.at[0]), pltpu.make_async_copy(cu_h, cu, sems.at[1])]
    start(*copies)
    south, north = field_packs(yn_r), field_packs(ys_r)
    low = lane_ids((NX, LANES)) < 64
    xs[0] = xw_r[0:XF, :].astype(f32)
    xs[1] = xe_r[0:XF, :].astype(f32)

    def edge_col(plane):
        return jnp.where(low, unpack_north(north, plane), unpack_south(south, plane))

    for c in range(4):
        mask[c, OWN, :] = jnp.broadcast_to(column(table[LAND + c : LAND + c + 1, 0:NX]), (NX, LANES))
    mask[4, OWN, :] = edge_col(MASK_PLANE) * jnp.where(low, inside("gy", False), inside("gy", True))
    in_west, in_east = inside("gx", True), inside("gx", False)
    for c in range(5):
        at = c * XPLANE + MASK_PLANE * 4
        mask[c, EAST, :] = xs[0, at : at + 4, :] * in_east
        mask[c, WEST, :] = xs[1, at : at + 4, :] * in_west
    lane = lane_ids((5, 8, LANES))
    for r in range(8, 48, 8):
        rows, m = slice(r, r + 8), mask[:, r : r + 8, :]
        around = mask[:, r + 1 : r + 9, :] + mask[:, r - 1 : r + 7, :] + lane_next(m, lane) + lane_prev(m, lane)
        coef[:, rows, :] = m * (1.0 - DIFFUSION * around)

    wait(*copies)
    for plane, (kind, c, level) in enumerate(PLANES):
        source, target = (tr, g0) if kind == "t" else (cu, vel)
        for col in range(5):
            if col < 4:
                body = source[c, level, :, col * LANES : (col + 1) * LANES]
            else:
                body = edge_col(plane)
            target[c, level, col, OWN, :] = body * mask[col, OWN, :]
            at = col * XPLANE + plane * 4
            target[c, level, col, EAST, :] = xs[0, at : at + 4, :] * mask[col, EAST, :]
            target[c, level, col, WEST, :] = xs[1, at : at + 4, :] * mask[col, WEST, :]

    sweep(g0, g1, vel, mask, coef, (4, 12), 3, 4, 3)
    sweep(g1, g2, vel, mask, coef, (5, 11), 4, 5, 3)
    finish(g2, done, vel, mask, coef, (6, 10), 5, 6, 3, tr, 3)


def outer_kernel(
    tr, g0, vel, g1, g2, mask, coef, zu_r, zd_r, z2u_r, z2d_r, ext, after, done, ocean_flux,
    s0, s1, s2, sv, before, sems,
):
    copies = [
        pltpu.make_async_copy(tr.at[:, pl.ds(0, 3)], before.at[0], sems.at[0]),
        pltpu.make_async_copy(tr.at[:, pl.ds(NL - 3, 3)], before.at[1], sems.at[1]),
        pltpu.make_async_copy(ext.at[:, :, pl.ds(0, 512)], ocean_flux, sems.at[2]),
    ]
    start(*copies)
    low = lane_ids((NX, LANES)) < 64
    for c in range(2):
        for k in range(2):
            s0[0, c, 3 + k] = g0[c, k]
            s0[1, c, k] = g0[c, 8 + k]
            s1[0, c, 3 + k] = g1[c, k]
            s1[1, c, k] = g1[c, 6 + k]
            s2[0, c, 3 + k] = g2[c, k]
            s2[1, c, k] = g2[c, 4 + k]
        for k in range(3):
            sv[0, c, 2 + k] = vel[c, k]
            sv[1, c, k] = vel[c, 7 + k]
    for got, z, face in ((z2d_r, zd_r, 0), (z2u_r, zu_r, 1)):
        z_south = (got[320:352, :].astype(f32),)
        z_north = (got[352:384, :].astype(f32),)
        halo = [[got[(s * 5 + c) * 32 : (s * 5 + c + 1) * 32, :].astype(f32) for c in range(5)] for s in (0, 1)]

        def put(target, body, near, plane, first):
            for col in range(4):
                target[col, OWN, :] = body[:, col * LANES : (col + 1) * LANES].astype(f32) * mask[col, OWN, :]
            if not near:
                return
            col4 = jnp.where(low, unpack_north(z_north, plane), unpack_south(z_south, plane))
            target[4, OWN, :] = col4 * mask[4, OWN, :]
            for col in range(5):
                target[col, EAST, :] = halo[0][col][first : first + 4] * mask[col, EAST, :]
                target[col, WEST, :] = halo[1][col][first : first + 4] * mask[col, WEST, :]

        for c in range(2):
            for k in range(3):
                near = k > 0 if face == 0 else k < 2
                level = 7 + k if face == 0 else k
                first = c * 8 + (k - 1 if face == 0 else k) * 4
                target = s0.at[face, c, k if face == 0 else 2 + k]
                put(target, z[c * 3 + k], near, PLANE_AT[("t", c, level)] if near else 0, first)
            for k in range(2):
                near = k == (1 if face == 0 else 0)
                level = 9 if face == 0 else 0
                first = 16 + c * 8 + (4 if face == 0 else 0)
                target = sv.at[face, c, k if face == 0 else 3 + k]
                put(target, z[6 + c * 2 + k], near, PLANE_AT[("c", c, level)], first)

    wait(copies[0], copies[1])
    for face in range(2):
        a, b, c, v = s0.at[face], s1.at[face], s2.at[face], sv.at[face]
        at0, at1, at2, atv = (0, 1, 2, 1) if face == 0 else (11, 10, 9, 10)
        last = (3, 6) if face == 0 else (10, 13)
        sweep(a, b, v, mask, coef, (1, 4) if face == 0 else (12, 15), at0, at1, atv)
        sweep(b, c, v, mask, coef, (2, 5) if face == 0 else (11, 14), at1, at2, atv)
        finish(c, done.at[face], v, mask, coef, last, at2, last[0], atv, before.at[face], last[0])
    wait(copies[2])


def surface_kernel(
    tr, g0, vel, g1, g2, mask, coef, ext, de_r, dw_r, middle, outer, out, s0, s1, s2, sv, before, top, sems
):
    sec = lax.axis_index("sec")
    writes = [
        pltpu.make_async_copy(outer.at[1], out.at[:, pl.ds(7, 3)], sems.at[0]),
        pltpu.make_async_copy(middle.at[:, pl.ds(1, 3)], out.at[:, pl.ds(4, 3)], sems.at[1]),
    ]
    start(*writes)

    @pl.when(sec != 0)
    def _():
        rest = [
            pltpu.make_async_copy(outer.at[0], out.at[:, pl.ds(0, 3)], sems.at[2]),
            pltpu.make_async_copy(middle.at[:, pl.ds(0, 1)], out.at[:, pl.ds(3, 1)], sems.at[3]),
        ]
        start(*rest)
        wait(*rest)

    @pl.when(sec == 0)
    def _():
        read = pltpu.make_async_copy(tr.at[:, pl.ds(0, 4)], before, sems.at[2])
        read.start()
        zero = jnp.zeros(PLANE, f32)
        for c in range(2):
            for target in (s0, s1, s2):
                target[c, 0] = zero
            for k in range(3):
                s0[c, 1 + k] = g0[c, k]
            for k in range(2):
                s1[c, 3 + k] = g1[c, 1 + k]
                s2[c, 4 + k] = g2[c, 1 + k]
            for k in range(4):
                sv[c, k] = vel[c, k]
        dw_f, de_f = dw_r[...].astype(f32), de_r[...].astype(f32)
        for f, (ref, at, gain) in enumerate(
            ((sv, (0, 0), WIND_GAIN), (sv, (1, 0), WIND_GAIN), (s0, (0, 1), HEAT_GAIN), (s0, (1, 1), -SALT_GAIN))
        ):
            for c in range(5):
                r = c * 16 + f * 4
                body = ext[f, :, c * LANES : (c + 1) * LANES]
                for rows, value in ((OWN, body), (EAST, dw_f[r : r + 4]), (WEST, de_f[r : r + 4])):
                    ref[at + (c, rows)] += gain * value * mask[c, rows, :]
        read.wait()
        sweep(s0, s1, sv, mask, coef, (3, 5), 2, 2, 3)
        sweep(s1, s2, sv, mask, coef, (3, 6), 2, 2, 3)
        finish(s2, top, sv, mask, coef, (3, 7), 2, 3, 3, before, 3)
        write = pltpu.make_async_copy(top, out.at[:, pl.ds(0, 4)], sems.at[3])
        write.start()
        write.wait()

    wait(*writes)


ANY = pl.BlockSpec(memory_space=pl.ANY)
HBM = pl.BlockSpec(memory_space=pltpu.HBM)
VMEM = pl.BlockSpec(memory_space=pltpu.VMEM)


def hbm(value):
    return pltpu.with_memory_space_constraint(value, pltpu.HBM)


def call(kernel, in_specs, outs, scratch, name, bytes_accessed, out_specs=None):
    return pl.pallas_call(
        kernel,
        out_shape=[jax.ShapeDtypeStruct(shape, dtype) for shape, dtype in outs],
        in_specs=in_specs,
        out_specs=out_specs or [VMEM] * len(outs),
        scratch_shapes=scratch,
        compiler_params=pltpu.CompilerParams(vmem_limit_bytes=VMEM_BYTES),
        cost_estimate=pl.CostEstimate(flops=0, bytes_accessed=bytes_accessed, transcendentals=0),
        name=name,
    )


def shifted(value, axis, step):
    count = lax.axis_size(axis)
    return lax.ppermute(value, axis, [(i, (i + step) % count) for i in range(count)])


def on_device(air_surface, remap_weights, sources, live_count, land_sea, tracers, currents):
    src = hbm(jnp.transpose(sources[:, :, 0, :], (1, 2, 0)))
    live = hbm(jnp.transpose(live_count, (1, 2, 0)))
    land = hbm(jnp.transpose(land_sea, (1, 0)))
    dma = pltpu.SemaphoreType.DMA

    yn, ys, flux, table = call(
        pack_y_kernel,
        [HBM] * 7,
        [((YROWS, LANES), bf16), ((YROWS, LANES), bf16), ((NT, 4, NX, LANES), bf16), ((16, LANES), f32)],
        [
            pltpu.VMEM((NT, 2, NX), jnp.int32),
            pltpu.VMEM((NT, 1, NX), jnp.int32),
            pltpu.VMEM((NT, NX), jnp.int32),
            pltpu.VMEM((NT, 5, NX, LANES), f32),
            pltpu.VMEM((NX, 2, 16, LANES), bf16),
            pltpu.VMEM((NX, 2, 16, LANES), bf16),
            pltpu.VMEM((192, LANES), f32),
            pltpu.VMEM((2, 2, 2, NL, NX, LANES), f32),
            dma((13,)),
        ],
        "pack_y",
        6_000_000,
    )(hbm(air_surface), src, live, land, hbm(remap_weights), hbm(tracers), hbm(currents))
    yn_r = shifted(yn, "gy", 1)
    ys_r = shifted(ys, "gy", -1)

    zu, zd = call(
        pack_z_kernel,
        [ANY, ANY, ANY],
        [((10, NX, 512), bf16)] * 2,
        [pltpu.VMEM((2, 2, 3, NX, 512), f32), pltpu.VMEM((2, 2, 2, NX, 512), f32), dma((4,))],
        "pack_z",
        3_000_000,
    )(tracers, currents, table)
    zu_r = shifted(zu, "sec", -1)
    zd_r = shifted(zd, "sec", 1)

    xe, xw = call(
        pack_x_kernel,
        [VMEM, VMEM, VMEM, VMEM, ANY, ANY],
        [((XROWS, LANES), bf16)] * 2,
        [pltpu.VMEM((XROWS, LANES), f32), pltpu.VMEM((2, 2, 2, NL, 8, 512), f32), dma((4,))],
        "pack_x",
        3_000_000,
    )(flux, yn_r, ys_r, table, tracers, currents)
    xe_r = shifted(xe, "gx", 1)
    xw_r = shifted(xw, "gx", -1)

    first_part, wedge = call(
        remap_kernel,
        [VMEM] * 4 + [ANY] * 2,
        [((5 * LANES, LANES), f32), ((2, NT, 2, LANES, LANES), bf16)],
        [
            pltpu.VMEM((8, 4, 48, LANES), f32),
            pltpu.VMEM((2 * NT, 2 * LANES, LANES), f32),
            pltpu.VMEM((NT, NX, 2, LANES, LANES), bf16),
            dma((8,)),
        ],
        "remap",
        18_000_000,
    )(flux, yn_r, ys_r, table, remap_weights, xe)
    part, send, z2u, z2d = call(
        rim_kernel,
        [VMEM] * 7,
        [((5 * LANES, LANES), f32), ((CROWS, LANES), bf16), ((ZROWS, LANES), bf16), ((ZROWS, LANES), bf16)],
        [],
        "rim",
        4_000_000,
    )(first_part, wedge, yn_r, ys_r, xe_r, xw_r, table)
    up_r = shifted(send, "sec", -1)
    down_r = shifted(send, "sec", 1)
    across_r = shifted(send, "sec", 2)
    z2u_r = shifted(z2u, "sec", -1)
    z2d_r = shifted(z2d, "sec", 1)

    plane = (5, 56, LANES)
    g0, vel, g1, g2, mask, coef, middle = call(
        middle_kernel,
        [ANY, ANY] + [VMEM] * 5 + [ANY] * 3,
        [
            ((2, NL) + plane, f32),
            ((2, NL) + plane, f32),
            ((2, NL - 2) + plane, f32),
            ((2, NL - 4) + plane, f32),
            (plane, f32),
            (plane, f32),
            ((2, NL - 6, NX, 512), f32),
        ],
        [
            pltpu.VMEM((2, NL, NX, 512), f32),
            pltpu.VMEM((2, NL, NX, 512), f32),
            pltpu.VMEM((2, XF, LANES), f32),
            dma((2,)),
        ],
        "middle",
        20_000_000,
    )(tracers, currents, yn_r, ys_r, xe_r, xw_r, table, send, zu_r, zd_r)

    ext, de, dw = call(
        flux_kernel,
        [VMEM] * 5,
        [((4, NX, 5 * LANES), f32), ((80, LANES), bf16), ((80, LANES), bf16)],
        [pltpu.VMEM((2, 80, LANES), f32)],
        "flux_sum",
        3_000_000,
    )(part, up_r, down_r, across_r, mask)
    de_r = shifted(de, "gx", 1)
    dw_r = shifted(dw, "gx", -1)

    outer, ocean_flux = call(
        outer_kernel,
        [ANY] + [VMEM] * 11 + [ANY],
        [((2, 2, 3, NX, 512), f32), ((4, NX, 512), f32)],
        [
            pltpu.VMEM((2, 2, 5) + plane, f32),
            pltpu.VMEM((2, 2, 5) + plane, f32),
            pltpu.VMEM((2, 2, 5) + plane, f32),
            pltpu.VMEM((2, 2, 5) + plane, f32),
            pltpu.VMEM((2, 2, 3, NX, 512), f32),
            dma((3,)),
        ],
        "outer",
        18_000_000,
        [VMEM, HBM],
    )(tracers, g0, vel, g1, g2, mask, coef, zu_r, zd_r, z2u_r, z2d_r, ext, de)

    (tracers_out,) = call(
        surface_kernel,
        [ANY] + [VMEM] * 11,
        [((2, NL, NX, 512), f32)],
        [
            pltpu.VMEM((2, 4) + plane, f32),
            pltpu.VMEM((2, 5) + plane, f32),
            pltpu.VMEM((2, 6) + plane, f32),
            pltpu.VMEM((2, 4) + plane, f32),
            pltpu.VMEM((2, 4, NX, 512), f32),
            pltpu.VMEM((2, 4, NX, 512), f32),
            dma((4,)),
        ],
        "surface",
        8_000_000,
        [HBM],
    )(tracers, g0, vel, g1, g2, mask, coef, ext, de_r, dw_r, middle, outer)
    return (tracers_out, ocean_flux)


def solution(mesh):
    return jax.shard_map(
        on_device,
        mesh=mesh,
        in_specs=(
            P(None, "gx", "gy", "sec", None),
            P("gx", "gy", "sec", None, None, None),
            P("gx", "gy", "sec", None),
            P("gx", "gy", "sec"),
            P("gx", "gy"),
            P(None, "sec", "gx", "gy"),
            P(None, "sec", "gx", "gy"),
        ),
        out_specs=(P(None, "sec", "gx", "gy"), P(None, "gx", "gy")),
        check_vma=False,
    )
```

```python
import jax
import jax.numpy as jnp
from jax import lax
from jax.experimental import pallas as pl
from jax.experimental.pallas import tpu as pltpu
from jax.sharding import PartitionSpec as P

f32 = jnp.float32
bf16 = jnp.bfloat16

DRAG = 0.6
WIND_GAIN = 0.5
HEAT_GAIN = 0.5
SALT_GAIN = 0.5
DIFFUSION = 0.15
ADVECTION = 0.5
VERTICAL = 0.2

NX = 32
NT = 4
NL = 10
LANES = 128

YF, YW, YC, YT, YROWS = 0, 256, 448, 464, 528
XPLANE, XP, XF, XROWS = 112, 448, 464, 496
CROWS, ZS, ZN, ZROWS = 528, 608, 640, 672
LAND = 8

VMEM_BYTES = 24 * 1024 * 1024

PLANES = (
    [("t", 0, level) for level in range(NL)]
    + [("t", 1, level) for level in range(NL)]
    + [("c", 0, 0), ("c", 0, 9), ("c", 1, 0), ("c", 1, 9)]
    + [("c", 0, level) for level in range(1, 9)]
    + [("c", 1, level) for level in range(1, 9)]
)
MASK_PLANE = len(PLANES)
PLANE_AT = {plane: index for index, plane in enumerate(PLANES)}


def x_rows(plane):
    if plane < 20:
        return 3 * plane, 3
    if plane < MASK_PLANE:
        return 60 + 2 * (plane - 20), 2
    return 100, 3


FACE_ROWS = (
    ("t", 0, 0, 0), ("t", 0, 0, 1), ("t", 0, 1, 0),
    ("t", 1, 0, 0), ("t", 1, 0, 1), ("t", 1, 1, 0),
    ("c", 0, 0, 0), ("c", 1, 0, 0),
)


def column(row):
    rows = lax.broadcasted_iota(jnp.int32, (NX, NX), 0)
    cols = lax.broadcasted_iota(jnp.int32, (NX, NX), 1)
    return jnp.sum(jnp.where(rows == cols, jnp.broadcast_to(row, (NX, NX)), 0.0), axis=1, keepdims=True)


def lane_ids(shape):
    return lax.broadcasted_iota(jnp.int32, shape, len(shape) - 1)


def start(*copies):
    for copy in copies:
        copy.start()


def wait(*copies):
    for copy in copies:
        copy.wait()


def roll(value, shift, axis):
    shift %= value.shape[axis]
    return value if shift == 0 else pltpu.roll(value, shift, axis)


def unpack_north(pack, plane, rows=slice(None)):
    return roll(pack[plane // 32][rows], -4 * (plane % 32), 1)


def unpack_south(pack, plane, rows=slice(None)):
    return roll(pack[plane // 32][rows], 4 * (plane % 32), 1)


def pack_y_kernel(
    air, src_h, live_h, land_h, w, tr, cu, yn, ys, flux, table, src, live, land, air_s, wn, ws, rows_s, edge, sems
):
    copies = [pltpu.make_async_copy(air, air_s, sems.at[0])]
    copies.append(pltpu.make_async_copy(w.at[:, NT - 1, 0, :, pl.ds(112, 16), :], wn, sems.at[1]))
    copies.append(pltpu.make_async_copy(w.at[:, 0, 0, :, pl.ds(0, 16), :], ws, sems.at[2]))
    for k, source in enumerate((tr, cu)):
        copies.append(pltpu.make_async_copy(source.at[:, :, :, pl.ds(384, 128)], edge.at[0, k], sems.at[3 + k]))
        copies.append(pltpu.make_async_copy(source.at[:, :, :, pl.ds(0, 128)], edge.at[1, k], sems.at[5 + k]))
    small = [
        pltpu.make_async_copy(source, target, sems.at[7 + k])
        for k, (source, target) in enumerate(((src_h, src), (live_h, live), (land_h, land)))
    ]
    start(copies[0], *small, *copies[1:])
    copies[0].wait()
    for t in range(NT):
        u, v, ta, qa, ts = (air_s[k, pl.ds(t, NX, stride=NT), :] for k in range(5))
        rate = DRAG * (1.0 + 0.5 * jnp.tanh(ts - ta)) * jnp.sqrt(u * u + v * v + 1.0)
        values = (rate * u, rate * v, rate * (ts - ta), rate * (jnp.exp(0.3 * ts) - qa))
        for f, value in enumerate(values):
            value = value.astype(bf16)
            flux[t, f] = value
            at = YF + ((t % 2) * 4 + f) * NX
            (ys if t < 2 else yn)[at : at + NX, :] = value
    wait(*small)
    slot = lax.broadcasted_iota(jnp.int32, (NT, 2, NX), 1)
    codes = jnp.where(slot < live[...], src[...], 9).astype(f32)
    table[...] = jnp.zeros((16, LANES), f32)
    for t in range(NT):
        table[2 * t : 2 * t + 2, 0:NX] = codes[t]
    table[LAND : LAND + NT, 0:NX] = land[...].astype(f32)
    sent = table[...].astype(bf16)
    yn[YC : YC + 16, :] = sent
    ys[YC : YC + 16, :] = sent
    wait(*copies[1:3])
    for send, tile, first in ((yn, wn, 13), (ys, ws, 0)):
        for x in range(NX):
            for s in range(2):
                block = tile[x, s].astype(f32)
                for d in range(3):
                    rows_s[pl.ds(d * 64 + s * 32 + x, 1), :] = block[first + d : first + d + 1]
        send[YW : YW + 192, :] = rows_s[...].astype(bf16)
    group = lane_ids((NX, LANES)) // 4
    packs = [[jnp.zeros((NX, LANES), f32)] * 2 for side in range(2)]
    for plane in range(MASK_PLANE + 1):
        if plane == 0:
            wait(copies[3], copies[4])
        if plane == 20:
            wait(copies[5], copies[6])
        part, at = plane // 32, plane % 32
        for side in range(2):
            if plane == MASK_PLANE:
                tile = LAND + (NT - 1 if side == 0 else 0)
                value = jnp.broadcast_to(column(table[tile : tile + 1, 0:NX]), (NX, LANES))
            else:
                kind, c, level = PLANES[plane]
                value = edge[side, 0 if kind == "t" else 1, c, level]
            turn, to = (-4 * at, 31 - at) if side == 0 else (4 * at, at)
            packs[side][part] = jnp.where(group == to, roll(value, turn, 1), packs[side][part])
    for send, halves in zip((yn, ys), packs):
        for part in range(2):
            send[YT + part * NX : YT + (part + 1) * NX, :] = halves[part].astype(bf16)


def pack_z_kernel(tr, cu, after, zu, zd, t_s, c_s, sems):
    copies = [
        pltpu.make_async_copy(tr.at[:, pl.ds(0, 3)], t_s.at[0], sems.at[0]),
        pltpu.make_async_copy(cu.at[:, pl.ds(0, 2)], c_s.at[0], sems.at[1]),
        pltpu.make_async_copy(tr.at[:, pl.ds(NL - 3, 3)], t_s.at[1], sems.at[2]),
        pltpu.make_async_copy(cu.at[:, pl.ds(NL - 2, 2)], c_s.at[1], sems.at[3]),
    ]
    for copy in copies:
        copy.start()
    for copy in copies:
        copy.wait()
    for side, send in enumerate((zu, zd)):
        for c in range(2):
            for level in range(3):
                send[c * 3 + level] = t_s[side, c, level].astype(bf16)
            for level in range(2):
                send[6 + c * 2 + level] = c_s[side, c, level].astype(bf16)


def inside(axis, low):
    at = lax.axis_index(axis)
    return jnp.where(at > 0 if low else at < lax.axis_size(axis) - 1, 1.0, 0.0).astype(f32)


def field_packs(y):
    return (y[YT : YT + NX, :].astype(f32), y[YT + NX : YT + 2 * NX, :].astype(f32))


def edge_packs(xw, xe):
    east, west = xw[XP : XP + 16, :].astype(f32), xe[XP : XP + 16, :].astype(f32)
    packs = [jnp.concatenate([east[4 * k : 4 * k + 4], west[4 * k : 4 * k + 4]], axis=0) for k in range(4)]
    return packs[:2], packs[2:]


def pack_x_kernel(flux, yn_r, ys_r, table, tr, cu, xe, xw, rows_s, edge, sems):
    copies = []
    for k, source in enumerate((tr, cu)):
        copies.append(pltpu.make_async_copy(source.at[:, :, pl.ds(0, 8), :], edge.at[0, k], sems.at[2 * k]))
        copies.append(pltpu.make_async_copy(source.at[:, :, pl.ds(24, 8), :], edge.at[1, k], sems.at[2 * k + 1]))
    start(*copies)
    packs = [*field_packs(yn_r), *field_packs(ys_r)]
    masks = [column(table[LAND + t : LAND + t + 1, 0:NX]) for t in range(NT)]
    in_south, in_north = inside("gy", True), inside("gy", False)
    for side, send in enumerate((xw, xe)):
        x = 0 if side == 0 else NX - 1
        first = 0 if side == 0 else NX - 4
        pack = jnp.concatenate([value[first : first + 4] for value in packs], axis=0)
        send[XP : XP + 16, :] = pack.astype(bf16)
        for t in range(8):
            for f in range(4):
                if 2 <= t < 6:
                    block = flux[t - 2, f].astype(f32)
                else:
                    got, half = (yn_r, t) if t < 2 else (ys_r, t - 6)
                    at = YF + (half * 4 + f) * NX
                    block = got[at : at + NX, :].astype(f32) * (in_south if t < 2 else in_north)
                rows_s[t * 4 + f : t * 4 + f + 1, :] = block[x : x + 1]
        send[XF:XROWS, :] = rows_s[0:32, :].astype(bf16)
    wait(*copies)
    for side, send in enumerate((xw, xe)):
        rows = slice(0, 8) if side == 0 else slice(24, 32)
        for c in range(4):
            for plane in range(MASK_PLANE + 1):
                if plane == MASK_PLANE:
                    value = jnp.broadcast_to(masks[c][rows], (8, LANES))
                else:
                    kind, component, level = PLANES[plane]
                    value = edge[side, 0 if kind == "t" else 1, component, level, :, c * LANES : (c + 1) * LANES]
                first, count = x_rows(plane)
                keep = slice(0, count) if side == 0 else slice(8 - count, 8)
                rows_s[c * XPLANE + first : c * XPLANE + first + count, :] = value[keep]
        send[0:XP, :] = rows_s[...].astype(bf16)


def remap_kernel(flux, yn_r, ys_r, table, w, after_x, part, wedge, rim, blk):
    zero = jnp.zeros((8, LANES), f32)
    in_south, in_north = inside("gy", True), inside("gy", False)
    for t in range(8):
        for f in range(4):
            if 2 <= t < 6:
                block = flux[t - 2, f].astype(f32)
            else:
                got, half = (yn_r, t) if t < 2 else (ys_r, t - 6)
                at = YF + (half * 4 + f) * NX
                block = got[at : at + NX, :].astype(f32) * (in_south if t < 2 else in_north)
            rim[t, f, 0:8, :] = zero
            rim[t, f, 8 : 8 + NX, :] = block
            rim[t, f, 8 + NX : 16 + NX, :] = zero

    def blocks(tile, row):
        code = jnp.broadcast_to(column(row), (NX, LANES))
        picked = [code == float(k) for k in range(9)]
        result = []
        for f in range(4):
            block = jnp.zeros((NX, LANES), f32)
            for k in range(9):
                x0 = 7 + k // 3
                block = jnp.where(picked[k], rim[tile + 2 + k % 3 - 1, f, x0 : x0 + NX, :], block)
            result.append(block)
        return result

    for t in range(NT):
        for s in range(2):
            row = 2 * t + s
            for f, block in enumerate(blocks(t, table[row : row + 1, 0:NX])):
                blk[row, f * NX : (f + 1) * NX, :] = block

    lane = lane_ids((NX, LANES))
    edges = [jnp.zeros((NX, LANES), f32) for f in range(4)]
    for got, tile, row, at in ((yn_r, -1, 6, 125), (ys_r, NT, 0, 0)):
        codes = got[YC : YC + 16, :].astype(f32)
        picked = [blocks(tile, codes[row + s : row + s + 1, 0:NX]) for s in range(2)]
        for d in range(3):
            weight = [
                got[YW + (d * 2 + s) * NX : YW + (d * 2 + s + 1) * NX, :].astype(f32) for s in range(2)
            ]
            for f in range(4):
                total = jnp.sum(weight[0] * picked[0][f] + weight[1] * picked[1][f], axis=1, keepdims=True)
                edges[f] = jnp.where(lane == at + d, total, edges[f])
    for f in range(4):
        part[4 * LANES + f * NX : 4 * LANES + (f + 1) * NX, :] = edges[f]

    for t in range(NT):

        def pair(i, _, t=t):
            x = 2 * i
            rows = [
                jnp.concatenate([blk[2 * t + s, pl.ds(x + j, 8, stride=NX), :] for j in range(2)], axis=0)
                for s in range(2)
            ]
            weights = jnp.concatenate(
                [jnp.concatenate([w[x + j, t, 0, s] for s in range(2)], axis=1) for j in range(2)], axis=0
            )
            product = lax.dot_general(
                jnp.concatenate(rows, axis=1).astype(bf16),
                weights,
                (((1,), (1,)), ((), ())),
                preferred_element_type=f32,
            )
            for j in range(2):
                block = product[8 * j : 8 * j + 4, j * LANES : (j + 1) * LANES]
                part[pl.ds(t * LANES + x + j, 4, stride=NX), :] = block
            return 0

        lax.fori_loop(0, NX // 2, pair, 0, unroll=8)
        for side, x in enumerate((0, NX - 1)):
            for s in range(2):
                wedge[side, t, s] = w[x, t, 0, s]


def rim_kernel(first_part, wedge, yn_r, ys_r, xe_r, xw_r, table, part, up, down, across, xs, rows_s):
    part[...] = first_part[...]
    near = [got[XF : XF + 32, :].astype(f32) * inside("gx", side == 0) for side, got in enumerate((xe_r, xw_r))]

    def blocks(side, tile, codes, row):
        x = 0 if side == 0 else NX - 1
        code = jnp.broadcast_to(codes[row : row + 1, x : x + 1], (4, LANES))
        block = jnp.zeros((4, LANES), f32)
        for k in range(3):
            at = (tile + 1 + k) * 4
            block = jnp.where(code == float(6 * side + k), near[side][at : at + 4], block)
        return block

    own_codes = table[...]
    gap = jnp.zeros((4, LANES), f32)
    for t in range(NT):
        rows = [
            jnp.concatenate([blocks(0, t, own_codes, 2 * t + s), gap, blocks(1, t, own_codes, 2 * t + s), gap], axis=0)
            for s in range(2)
        ]
        weights = jnp.concatenate(
            [jnp.concatenate([wedge[side, t, s] for s in range(2)], axis=1) for side in range(2)], axis=0
        )
        product = lax.dot_general(
            jnp.concatenate(rows, axis=1).astype(bf16), weights, (((1,), (1,)), ((), ())), preferred_element_type=f32
        )
        for side, x in enumerate((0, NX - 1)):
            part[pl.ds(t * LANES + x, 4, stride=NX), :] += product[8 * side : 8 * side + 4, side * LANES : (side + 1) * LANES]
    lane = lane_ids((4, LANES))
    for side, x in enumerate((0, NX - 1)):
        added = jnp.zeros((4, LANES), f32)
        for got, tile, row, at in ((yn_r, -1, 6, 125), (ys_r, NT, 0, 0)):
            codes = got[YC : YC + 16, :].astype(f32)
            picked = [blocks(side, tile, codes, row + s) for s in range(2)]
            for d in range(3):
                total = jnp.zeros((4, LANES), f32)
                for s in range(2):
                    first = YW + (d * 2 + s) * NX
                    weight = got[first : first + NX, :].astype(f32)[x : x + 1]
                    total += weight * picked[s]
                added = jnp.where(lane == at + d, jnp.sum(total, axis=1, keepdims=True), added)
        part[pl.ds(4 * LANES + x, 4, stride=NX), :] += added

    turned = part[4 * LANES : 5 * LANES, :].T
    halo = jnp.concatenate([turned[0:8], turned[LANES - 8 :]], axis=0).astype(bf16)
    own = part[0 : 4 * LANES, :].astype(bf16)
    for send in (up, down, across):
        send[0 : 4 * LANES, :] = own
        send[4 * LANES : CROWS, :] = halo
    xs[0] = xw_r[0:XP, :].astype(f32)
    xs[1] = xe_r[0:XP, :].astype(f32)
    south, north = edge_packs(xw_r, xe_r)
    low = lane_ids((8, LANES)) < 64
    for send, levels in ((up, (0, 1)), (down, (NL - 1, NL - 2))):
        for k, (kind, component, depth, column_at) in enumerate(FACE_ROWS):
            plane = PLANE_AT[(kind, component, levels[depth])]
            first, count = x_rows(plane)
            for c in range(4):
                for side in range(2):
                    at = c * XPLANE + first + (column_at if side == 0 else count - 1 - column_at)
                    to = c * 16 + side * 8 + k
                    rows_s[to : to + 1, :] = xs[side, at : at + 1, :]
            edge_col = jnp.where(low, unpack_north(north, plane), unpack_south(south, plane))
            for side in range(2):
                at = column_at if side == 0 else 7 - column_at
                to = 64 + side * 8 + k
                rows_s[to : to + 1, :] = edge_col[at : at + 1]
        send[CROWS:ZS, :] = rows_s[...].astype(bf16)
        send[ZS:ZN, :] = yn_r[YT : YT + NX, :]
        send[ZN:ZROWS, :] = ys_r[YT : YT + NX, :]


def flux_kernel(part, up_r, down_r, across_r, grid, ext, de, dw, rows_s):
    got = [ref[4 * LANES : CROWS, :].astype(f32) for ref in (up_r, down_r, across_r)]
    turned = got[0] + got[1] + got[2]
    halo = jnp.concatenate([turned[0:8], jnp.zeros((LANES - 16, LANES), f32), turned[8:16]], axis=0).T
    for c in range(5):
        for f in range(4):
            at = c * LANES + f * NX
            total = part[at : at + NX, :]
            if c < 4:
                for ref in (up_r, down_r, across_r):
                    total = total + ref[at : at + NX, :].astype(f32)
            else:
                total = total + halo[f * NX : (f + 1) * NX]
            total = total * grid[MASK, c, OWN, :]
            ext[f, :, c * LANES : (c + 1) * LANES] = total
            rows_s[0, c * 16 + f * 4 : c * 16 + f * 4 + 4, :] = total[0:4]
            rows_s[1, c * 16 + f * 4 : c * 16 + f * 4 + 4, :] = total[NX - 4 : NX]
    dw[...] = rows_s[0].astype(bf16)
    de[...] = rows_s[1].astype(bf16)


def lane_next(value, lane):
    rolled = pltpu.roll(value, LANES - 1, 2)
    return jnp.where(lane == LANES - 1, jnp.concatenate([rolled[1:], rolled[:1]], axis=0), rolled)


def lane_prev(value, lane):
    rolled = pltpu.roll(value, 1, 2)
    return jnp.where(lane == 0, jnp.concatenate([rolled[-1:], rolled[:-1]], axis=0), rolled)


OWN, WEST, EAST = slice(12, 44), slice(8, 12), slice(44, 48)
PLANE = (5, 56, LANES)


MASK, BASE, VERT, KEPT = range(4)


def advance(here, above, below, velocity, grid, rows, open_below=None):
    r = rows.start
    lane = lane_ids((5, 8, LANES))

    def at(plane, c, where=rows):
        return plane[0][c, plane[1], :, where, :]

    base, vert, kept = (grid[k, :, rows, :] for k in (BASE, VERT, KEPT))
    if above is None:
        kept = kept + vert
    if open_below is not None:
        down = vert * open_below
        kept = kept + (vert - down)
    a, b = at(velocity, 0), at(velocity, 1)
    east, west, north, south = base - a, base + a, base - b, base + b
    results = []
    for c in range(2):
        g = at(here, c)
        new = kept * g
        new += east * at(here, c, slice(r + 1, r + 9)) + west * at(here, c, slice(r - 1, r + 7))
        new += north * lane_next(g, lane) + south * lane_prev(g, lane)
        if above is None:
            new += vert * at(below, c)
        elif open_below is None:
            new += vert * (at(above, c) + at(below, c))
        else:
            new += vert * at(above, c) + down * at(below, c)
        results.append(new)
    return results


def land_or(value, grid, rows, tr, c, level, x, out):
    for col in range(4):
        cells = slice(col * LANES, (col + 1) * LANES)
        out[:, cells] = jnp.where(grid[MASK, col, rows, :] > 0.0, value[col], tr[c, level, x : x + 8, cells])


def middle_kernel(
    tr, cu, yn_r, ys_r, xe_r, xw_r, table, after, after_zu, after_zd, g0, vel, g1, g2, grid, done, xs
):
    south, north = field_packs(yn_r), field_packs(ys_r)
    low = lane_ids((NX, LANES)) < 64
    edge_south, edge_north = edge_packs(xw_r, xe_r)
    edge_low = lane_ids((8, LANES)) < 64
    xs[0] = xw_r[0:XP, :].astype(f32)
    xs[1] = xe_r[0:XP, :].astype(f32)
    in_south, in_north, in_west, in_east = inside("gy", True), inside("gy", False), inside("gx", True), inside("gx", False)

    def pieces(plane, col, own):
        first, count = x_rows(plane)
        if col < 4:
            at = col * XPLANE + first
            east, west = xs[0, at : at + count, :], xs[1, at : at + count, :]
        else:
            own = jnp.where(low, unpack_north(north, plane), unpack_south(south, plane))
            edge = jnp.where(edge_low, unpack_north(edge_north, plane), unpack_south(edge_south, plane))
            east, west = edge[0:count], edge[8 - count : 8]
        return ((OWN, own), (slice(44, 44 + count), east), (slice(12 - count, 12), west))

    for col in range(5):
        own = None
        if col < 4:
            own = jnp.broadcast_to(column(table[LAND + col : LAND + col + 1, 0:NX]), (NX, LANES))
        for (rows, value), in_x in zip(pieces(MASK_PLANE, col, own), (1.0, in_east, in_west)):
            if col == 4:
                value = value * jnp.where(low[0 : value.shape[0]], in_north, in_south)
            grid[MASK, col, rows, :] = value * in_x
    lane = lane_ids((5, 8, LANES))
    for r in range(8, 48, 8):
        rows, m = slice(r, r + 8), grid[MASK, :, r : r + 8, :]
        around = grid[MASK, :, r + 1 : r + 9, :] + grid[MASK, :, r - 1 : r + 7, :] + lane_next(m, lane) + lane_prev(m, lane)
        grid[BASE, :, rows, :] = DIFFUSION * m
        grid[VERT, :, rows, :] = VERTICAL * m
        grid[KEPT, :, rows, :] = m * (1.0 - 2.0 * VERTICAL - DIFFUSION * around)

    for col in range(5):
        for plane, (kind, c, level) in enumerate(PLANES):
            source, target = (tr, g0) if kind == "t" else (cu, vel)
            own = source[c, level, :, col * LANES : (col + 1) * LANES] if col < 4 else None
            for rows, value in pieces(plane, col, own):
                scale = grid[MASK, col, rows, :]
                target[c, level, col, rows, :] = value * (scale if kind == "t" else ADVECTION * scale)

    def sweep(src, src_at, dst, dst_at, levels):
        def one_level(l, _):
            for r in range(8, 48, 8):
                rows = slice(r, r + 8)
                at = l - src_at
                step = advance((src, at), (src, at - 1), (src, at + 1), (vel, l - 3), grid, rows)
                for c, value in enumerate(step):
                    dst[c, l - dst_at, :, rows, :] = value
            return 0

        lax.fori_loop(levels[0], levels[1], one_level, 0, unroll=2)

    sweep(g0, 3, g1, 4, (4, 12))
    sweep(g1, 4, g2, 5, (5, 11))

    def last(l, _):
        for r in range(12, 44, 8):
            rows = slice(r, r + 8)
            at = l - 5
            step = advance((g2, at), (g2, at - 1), (g2, at + 1), (vel, l - 3), grid, rows)
            for c, value in enumerate(step):
                land_or(value, grid, rows, tr, c, l - 3, r - 12, done.at[c, l - 6, r - 12 : r - 4])
        return 0

    lax.fori_loop(6, 10, last, 0, unroll=2)


def face_steps(planes, velocities, levels, out, grid, tr, starts, last_starts, out_x=lambda x: x, open_below=None):
    for k in range(3):
        for l in levels[k]:
            here, above, below = (planes[k].get(i) for i in (l, l - 1, l + 1))
            floor = open_below if l == 12 else None
            for r in starts if k < 2 else last_starts:
                rows = slice(r, r + 8)
                step = advance(here, above, below, velocities[l], grid, rows, floor)
                for c, value in enumerate(step):
                    if k < 2:
                        ref, index = planes[k + 1][l]
                        ref[c, index, :, rows, :] = value
                    else:
                        x = r - 12
                        land_or(value, grid, rows, tr, c, l - 3, x, out.at[c, l - levels[2][0], out_x(x) : out_x(x) + 8])


def planes_of(*runs):
    return {first + k: (ref, index + k) for first, count, ref, index in runs for k in range(count)}


def forced(velocities, tracers):
    return (
        (velocities, 0, ADVECTION * WIND_GAIN),
        (velocities, 1, ADVECTION * WIND_GAIN),
        (tracers, 0, HEAT_GAIN),
        (tracers, 1, -SALT_GAIN),
    )


WHOLE, INNER = range(8, 48, 8), range(12, 44, 8)


def outer_kernel(
    tr, g0, vel, g1, g2, grid, zu_r, zd_r, up_r, down_r, ext, middle, after, out, ocean_flux, s0, sv, s1, s2,
    b0, bv, b1, b2, top, bottom, sems,
):
    sec = lax.axis_index("sec")
    writes = [
        pltpu.make_async_copy(ext.at[:, :, pl.ds(0, 512)], ocean_flux, sems.at[0]),
        pltpu.make_async_copy(middle.at[:, pl.ds(1, 3)], out.at[:, pl.ds(4, 3)], sems.at[1]),
        pltpu.make_async_copy(bottom, out.at[:, pl.ds(7, 3)], sems.at[2]),
    ]
    start(*writes[:2])
    low = lane_ids((NX, LANES)) < 64

    def halo_planes(got, z, face, tracers, velocities):
        z_south = (got[ZS:ZN, :].astype(f32),)
        z_north = (got[ZN:ZROWS, :].astype(f32),)
        near = [got[CROWS + c * 16 : CROWS + (c + 1) * 16, :].astype(f32) for c in range(5)]

        def put(target, body, plane, at, scale):
            for col in range(4):
                value = body[:, col * LANES : (col + 1) * LANES].astype(f32)
                target[col, OWN, :] = value * (scale * grid[MASK, col, OWN, :])
            if plane is None:
                return
            col4 = jnp.where(low, unpack_north(z_north, plane), unpack_south(z_south, plane))
            target[4, OWN, :] = col4 * (scale * grid[MASK, 4, OWN, :])
            for col in range(5):
                for k, row in enumerate(at):
                    for to, value in ((44 + k, near[col][row : row + 1]), (11 - k, near[col][8 + row : 9 + row])):
                        target[col, to : to + 1, :] = value * (scale * grid[MASK, col, to : to + 1, :])

        for c in range(2):
            for k in range(3):
                depth = k if face == 1 else 2 - k
                level = k if face == 1 else 7 + k
                plane = PLANE_AT[("t", c, level)] if depth < 2 else None
                at = (3 * c, 3 * c + 1) if depth == 0 else (3 * c + 2,)
                put(tracers.at[c, k], z[c * 3 + k], plane, at, 1.0)
            for k in range(2):
                depth = k if face == 1 else 1 - k
                plane = PLANE_AT[("c", c, 0 if face == 1 else 9)] if depth == 0 else None
                put(velocities.at[c, k], z[6 + c * 2 + k], plane, (6 + c,), ADVECTION)

    halo_planes(up_r, zu_r, 1, b0, bv)
    face_steps(
        (
            planes_of((11, 2, g0, 8), (13, 3, b0, 0)),
            planes_of((10, 2, g1, 6), (12, 3, b1, 0)),
            planes_of((9, 2, g2, 4), (11, 3, b2, 0)),
        ),
        planes_of((10, 3, vel, 7), (13, 2, bv, 0)),
        (range(12, 15), range(11, 14), range(10, 13)),
        bottom, grid, tr, WHOLE, INNER,
        open_below=jnp.where(sec < lax.axis_size("sec") - 1, 1.0, 0.0).astype(f32),
    )
    writes[2].start()

    @pl.when(sec != 0)
    def _():
        level3 = pltpu.make_async_copy(middle.at[:, pl.ds(0, 1)], out.at[:, pl.ds(3, 1)], sems.at[3])
        level3.start()
        halo_planes(down_r, zd_r, 0, s0, sv)
        face_steps(
            (
                planes_of((0, 3, s0, 0), (3, 2, g0, 0)),
                planes_of((1, 3, s1, 0), (4, 2, g1, 0)),
                planes_of((2, 3, s2, 0), (5, 2, g2, 0)),
            ),
            planes_of((1, 2, sv, 0), (3, 3, vel, 0)),
            (range(1, 4), range(2, 5), range(3, 6)),
            top, grid, tr, WHOLE, INNER,
        )
        write = pltpu.make_async_copy(top.at[:, pl.ds(0, 3)], out.at[:, pl.ds(0, 3)], sems.at[4])
        write.start()
        wait(level3, write)

    @pl.when(sec == 0)
    def _():
        for f, (ref, c, gain) in enumerate(forced(sv, s0)):
            source = vel if f < 2 else g0
            for col in range(5):
                for r in range(8, 48, 8):
                    ref[c, 0, col, r : r + 8, :] = source[c, 0, col, r : r + 8, :]
                ref[c, 0, col, OWN, :] += gain * ext[f, :, col * LANES : (col + 1) * LANES] * grid[MASK, col, OWN, :]
        face_steps(
            surface_planes(s0, s1, s2, g0, g1, g2),
            planes_of((3, 1, sv, 0), (4, 3, vel, 1)),
            SURFACE_LEVELS,
            top, grid, tr, WHOLE, INNER,
        )
        write = pltpu.make_async_copy(top, out.at[:, pl.ds(0, 4)], sems.at[3])
        write.start()
        write.wait()

    wait(*writes)


SURFACE_LEVELS = (range(3, 5), range(3, 6), range(3, 7))


def surface_planes(s0, s1, s2, g0, g1, g2):
    return (
        planes_of((3, 1, s0, 0), (4, 2, g0, 1)),
        planes_of((3, 2, s1, 0), (5, 2, g1, 1)),
        planes_of((3, 3, s2, 0), (6, 2, g2, 1)),
    )


def surface_kernel(
    unfinished, tr, s0, sv, s1, s2, g0, vel, g1, g2, grid, de_r, dw_r, out, e0, ev, e1, e2, edge, sems
):
    @pl.when(lax.axis_index("sec") == 0)
    def _():
        halo = (de_r[...].astype(f32), dw_r[...].astype(f32))
        for c in range(2):
            for target, source, planes, groups in (
                (e0, s0, 1, (8, 16, 32, 40)),
                (ev, sv, 1, (8, 16, 32, 40)),
                (e1, s1, 2, (16, 32)),
                (e2, s2, 3, (16, 32)),
            ):
                for k in range(planes):
                    for r in groups:
                        target[c, k, :, r : r + 8, :] = source[c, k, :, r : r + 8, :]
        for side, rows in enumerate((WEST, EAST)):
            for f, (ref, c, gain) in enumerate(forced(ev, e0)):
                for col in range(5):
                    r = col * 16 + f * 4
                    ref[c, 0, col, rows, :] += gain * halo[side][r : r + 4] * grid[MASK, col, rows, :]
        face_steps(
            surface_planes(e0, e1, e2, g0, g1, g2),
            planes_of((3, 1, ev, 0), (4, 3, vel, 1)),
            SURFACE_LEVELS,
            edge, grid, tr, (8, 40), (12, 36), lambda x: 0 if x == 0 else 8,
        )
        writes = [
            pltpu.make_async_copy(
                edge.at[:, :, pl.ds(8 * side, 8)], out.at[:, pl.ds(0, 4), pl.ds(24 * side, 8)], sems.at[side]
            )
            for side in range(2)
        ]
        start(*writes)
        wait(*writes)


ANY = pl.BlockSpec(memory_space=pl.ANY)
HBM = pl.BlockSpec(memory_space=pltpu.HBM)
VMEM = pl.BlockSpec(memory_space=pltpu.VMEM)


def hbm(value):
    return pltpu.with_memory_space_constraint(value, pltpu.HBM)


def call(kernel, in_specs, outs, scratch, name, bytes_accessed, out_specs=None, aliases=None):
    return pl.pallas_call(
        kernel,
        out_shape=[jax.ShapeDtypeStruct(shape, dtype) for shape, dtype in outs],
        in_specs=in_specs,
        out_specs=out_specs or [VMEM] * len(outs),
        scratch_shapes=scratch,
        input_output_aliases=aliases or {},
        compiler_params=pltpu.CompilerParams(vmem_limit_bytes=VMEM_BYTES),
        cost_estimate=pl.CostEstimate(flops=0, bytes_accessed=bytes_accessed, transcendentals=0),
        name=name,
    )


def shifted(value, axis, step):
    count = lax.axis_size(axis)
    return lax.ppermute(value, axis, [(i, (i + step) % count) for i in range(count)])


def on_device(air_surface, remap_weights, sources, live_count, land_sea, tracers, currents):
    src = hbm(jnp.transpose(sources[:, :, 0, :], (1, 2, 0)))
    live = hbm(jnp.transpose(live_count, (1, 2, 0)))
    land = hbm(jnp.transpose(land_sea, (1, 0)))
    dma = pltpu.SemaphoreType.DMA

    yn, ys, flux, table = call(
        pack_y_kernel,
        [HBM] * 7,
        [((YROWS, LANES), bf16), ((YROWS, LANES), bf16), ((NT, 4, NX, LANES), bf16), ((16, LANES), f32)],
        [
            pltpu.VMEM((NT, 2, NX), jnp.int32),
            pltpu.VMEM((NT, 1, NX), jnp.int32),
            pltpu.VMEM((NT, NX), jnp.int32),
            pltpu.VMEM((5, NX * NT, LANES), f32),
            pltpu.VMEM((NX, 2, 16, LANES), bf16),
            pltpu.VMEM((NX, 2, 16, LANES), bf16),
            pltpu.VMEM((192, LANES), f32),
            pltpu.VMEM((2, 2, 2, NL, NX, LANES), f32),
            dma((10,)),
        ],
        "pack_y",
        6_000_000,
    )(hbm(air_surface.reshape(5, NX * NT, LANES)), src, live, land, hbm(remap_weights), hbm(tracers), hbm(currents))
    yn_r = shifted(yn, "gy", 1)
    ys_r = shifted(ys, "gy", -1)

    zu, zd = call(
        pack_z_kernel,
        [ANY, ANY, ANY],
        [((10, NX, 512), bf16)] * 2,
        [pltpu.VMEM((2, 2, 3, NX, 512), f32), pltpu.VMEM((2, 2, 2, NX, 512), f32), dma((4,))],
        "pack_z",
        3_000_000,
    )(tracers, currents, table)
    zu_r = shifted(zu, "sec", -1)
    zd_r = shifted(zd, "sec", 1)

    xe, xw = call(
        pack_x_kernel,
        [VMEM, VMEM, VMEM, VMEM, ANY, ANY],
        [((XROWS, LANES), bf16)] * 2,
        [pltpu.VMEM((XP, LANES), f32), pltpu.VMEM((2, 2, 2, NL, 8, 512), f32), dma((4,))],
        "pack_x",
        3_000_000,
    )(flux, yn_r, ys_r, table, tracers, currents)
    xe_r = shifted(xe, "gx", 1)
    xw_r = shifted(xw, "gx", -1)

    first_part, wedge = call(
        remap_kernel,
        [VMEM] * 5 + [ANY],
        [((5 * LANES, LANES), f32), ((2, NT, 2, LANES, LANES), bf16)],
        [
            pltpu.VMEM((8, 4, 48, LANES), f32),
            pltpu.VMEM((2 * NT, 2 * LANES, LANES), f32),
        ],
        "remap",
        18_000_000,
    )(flux, yn_r, ys_r, table, remap_weights, xe)
    part, up, down, across = call(
        rim_kernel,
        [VMEM] * 7,
        [((5 * LANES, LANES), f32), ((ZROWS, LANES), bf16), ((ZROWS, LANES), bf16), ((CROWS, LANES), bf16)],
        [pltpu.VMEM((2, XP, LANES), f32), pltpu.VMEM((80, LANES), f32)],
        "rim",
        4_000_000,
    )(first_part, wedge, yn_r, ys_r, xe_r, xw_r, table)
    up_r = shifted(up, "sec", -1)
    down_r = shifted(down, "sec", 1)
    across_r = shifted(across, "sec", 2)

    plane = (5, 56, LANES)
    g0, vel, g1, g2, grid, middle = call(
        middle_kernel,
        [VMEM] * 7 + [ANY] * 3,
        [
            ((2, NL) + plane, f32),
            ((2, NL) + plane, f32),
            ((2, NL - 2) + plane, f32),
            ((2, NL - 4) + plane, f32),
            ((4,) + plane, f32),
            ((2, NL - 6, NX, 512), f32),
        ],
        [
            pltpu.VMEM((2, XP, LANES), f32),
        ],
        "middle",
        20_000_000,
    )(tracers, currents, yn_r, ys_r, xe_r, xw_r, table, across, zu_r, zd_r)

    ext, de, dw = call(
        flux_kernel,
        [VMEM] * 5,
        [((4, NX, 5 * LANES), f32), ((80, LANES), bf16), ((80, LANES), bf16)],
        [pltpu.VMEM((2, 80, LANES), f32)],
        "flux_sum",
        3_000_000,
    )(part, up_r, down_r, across_r, grid)
    de_r = shifted(de, "gx", 1)
    dw_r = shifted(dw, "gx", -1)

    unfinished, ocean_flux, s0, sv, s1, s2 = call(
        outer_kernel,
        [VMEM] * 12 + [ANY],
        [((2, NL, NX, 512), f32), ((4, NX, 512), f32)] + [((2, count) + plane, f32) for count in (3, 2, 3, 3)],
        [pltpu.VMEM((2, count) + plane, f32) for count in (3, 2, 3, 3)]
        + [pltpu.VMEM((2, 4, NX, 512), f32), pltpu.VMEM((2, 3, NX, 512), f32), dma((5,))],
        "outer",
        18_000_000,
        [HBM, HBM] + [VMEM] * 4,
    )(tracers, g0, vel, g1, g2, grid, zu_r, zd_r, up_r, down_r, ext, middle, de)

    (tracers_out,) = call(
        surface_kernel,
        [HBM] + [VMEM] * 12,
        [((2, NL, NX, 512), f32)],
        [pltpu.VMEM((2, count) + plane, f32) for count in (1, 1, 2, 3)]
        + [pltpu.VMEM((2, 4, 16, 512), f32), dma((2,))],
        "surface",
        8_000_000,
        [HBM],
        {0: 0},
    )(unfinished, tracers, s0, sv, s1, s2, g0, vel, g1, g2, grid, de_r, dw_r)
    return (tracers_out, ocean_flux)


def solution(mesh):
    return jax.shard_map(
        on_device,
        mesh=mesh,
        in_specs=(
            P(None, "gx", "gy", "sec", None),
            P("gx", "gy", "sec", None, None, None),
            P("gx", "gy", "sec", None),
            P("gx", "gy", "sec"),
            P("gx", "gy"),
            P(None, "sec", "gx", "gy"),
            P(None, "sec", "gx", "gy"),
        ),
        out_specs=(P(None, "sec", "gx", "gy"), P(None, "gx", "gy")),
        check_vma=False,
    )
```

```python
import jax
import jax.numpy as jnp
from jax import lax
from jax.experimental import pallas as pl
from jax.experimental.pallas import tpu as pltpu
from jax.sharding import PartitionSpec as P

f32 = jnp.float32
bf16 = jnp.bfloat16

DRAG = 0.6
WIND_GAIN = 0.5
HEAT_GAIN = 0.5
SALT_GAIN = 0.5
DIFFUSION = 0.15
ADVECTION = 0.5
VERTICAL = 0.2

NX = 32
NT = 4
NL = 10
LANES = 128

YF, YW, YC, YT, YROWS = 0, 256, 448, 464, 496
XPLANE, XP, XF, XROWS = 112, 448, 464, 496
CROWS, ZP, ZROWS = 528, 608, 640
LAND = 8

VMEM_BYTES = 24 * 1024 * 1024

PLANES = (
    [("t", 0, level) for level in range(NL)]
    + [("t", 1, level) for level in range(NL)]
    + [("c", 0, 0), ("c", 0, 9), ("c", 1, 0), ("c", 1, 9)]
    + [("c", 0, level) for level in range(1, 9)]
    + [("c", 1, level) for level in range(1, 9)]
)
MASK_PLANE = len(PLANES)
PLANE_AT = {plane: index for index, plane in enumerate(PLANES)}


def x_rows(plane):
    if plane < 20:
        return 3 * plane, 3
    if plane < MASK_PLANE:
        return 60 + 2 * (plane - 20), 2
    return 100, 3


FACE_ROWS = (
    ("t", 0, 0, 0), ("t", 0, 0, 1), ("t", 0, 1, 0),
    ("t", 1, 0, 0), ("t", 1, 0, 1), ("t", 1, 1, 0),
    ("c", 0, 0, 0), ("c", 1, 0, 0),
)
APART = 6


def column(row):
    rows = lax.broadcasted_iota(jnp.int32, (NX, NX), 0)
    cols = lax.broadcasted_iota(jnp.int32, (NX, NX), 1)
    return jnp.sum(jnp.where(rows == cols, jnp.broadcast_to(row, (NX, NX)), 0.0), axis=1, keepdims=True)


def lane_ids(shape):
    return lax.broadcasted_iota(jnp.int32, shape, len(shape) - 1)


def start(*copies):
    for copy in copies:
        copy.start()


def wait(*copies):
    for copy in copies:
        copy.wait()


def even(axis):
    return lax.axis_index(axis) % 2 == 0


def sort_pair(axis, a, b, plus, minus):
    @pl.when(even(axis))
    def _():
        plus[...] = a[...]
        minus[...] = b[...]

    @pl.when(jnp.logical_not(even(axis)))
    def _():
        plus[...] = b[...]
        minus[...] = a[...]


def roll(value, shift, axis):
    shift %= value.shape[axis]
    return value if shift == 0 else pltpu.roll(value, shift, axis)


def unpack_north(pack, plane, rows=slice(None)):
    return roll(pack[rows], -3 * plane, 1)


def unpack_south(pack, plane, rows=slice(None)):
    return roll(pack[rows], 125 - 3 * plane, 1)


def pack_y_kernel(
    air, src_h, live_h, land_h, w, tr, cu, ya, yb, flux, table, yn, ys, src, live, land, air_s, wn, ws, rows_s, edge, sems
):
    copies = [pltpu.make_async_copy(air, air_s, sems.at[0])]
    copies.append(pltpu.make_async_copy(w.at[:, NT - 1, 0, :, pl.ds(112, 16), :], wn, sems.at[1]))
    copies.append(pltpu.make_async_copy(w.at[:, 0, 0, :, pl.ds(0, 16), :], ws, sems.at[2]))
    for k, source in enumerate((tr, cu)):
        copies.append(pltpu.make_async_copy(source.at[:, :, :, pl.ds(384, 128)], edge.at[0, k], sems.at[3 + k]))
        copies.append(pltpu.make_async_copy(source.at[:, :, :, pl.ds(0, 128)], edge.at[1, k], sems.at[5 + k]))
    small = [
        pltpu.make_async_copy(source, target, sems.at[7 + k])
        for k, (source, target) in enumerate(((src_h, src), (live_h, live), (land_h, land)))
    ]
    start(copies[0], *small, *copies[1:])
    copies[0].wait()
    for t in range(NT):
        u, v, ta, qa, ts = (air_s[k, pl.ds(t, NX, stride=NT), :] for k in range(5))
        rate = DRAG * (1.0 + 0.5 * jnp.tanh(ts - ta)) * jnp.sqrt(u * u + v * v + 1.0)
        values = (rate * u, rate * v, rate * (ts - ta), rate * (jnp.exp(0.3 * ts) - qa))
        for f, value in enumerate(values):
            value = value.astype(bf16)
            flux[t, f] = value
            at = YF + ((t % 2) * 4 + f) * NX
            (ys if t < 2 else yn)[at : at + NX, :] = value
    wait(*small)
    slot = lax.broadcasted_iota(jnp.int32, (NT, 2, NX), 1)
    codes = jnp.where(slot < live[...], src[...], 9).astype(f32)
    table[...] = jnp.zeros((16, LANES), f32)
    for t in range(NT):
        table[2 * t : 2 * t + 2, 0:NX] = codes[t]
    table[LAND : LAND + NT, 0:NX] = land[...].astype(f32)
    sent = table[...].astype(bf16)
    yn[YC : YC + 16, :] = sent
    ys[YC : YC + 16, :] = sent
    wait(*copies[1:3])
    for send, tile, first in ((yn, wn, 13), (ys, ws, 0)):
        for x in range(NX):
            for s in range(2):
                block = tile[x, s].astype(f32)
                for d in range(3):
                    rows_s[pl.ds(d * 64 + s * 32 + x, 1), :] = block[first + d : first + d + 1]
        send[YW : YW + 192, :] = rows_s[...].astype(bf16)
    group = lane_ids((NX, LANES)) // 3
    packs = [jnp.zeros((NX, LANES), f32)] * 2
    for plane in range(MASK_PLANE + 1):
        if plane == 0:
            wait(copies[3], copies[4])
        if plane == 20:
            wait(copies[5], copies[6])
        for side in range(2):
            if plane == MASK_PLANE:
                tile = LAND + (NT - 1 if side == 0 else 0)
                value = jnp.broadcast_to(column(table[tile : tile + 1, 0:NX]), (NX, LANES))
            else:
                kind, c, level = PLANES[plane]
                value = edge[side, 0 if kind == "t" else 1, c, level]
            turn = 3 * plane - (125 if side == 0 else 0)
            packs[side] = jnp.where(group == plane, roll(value, turn, 1), packs[side])
    for send, pack in zip((yn, ys), packs):
        send[YT : YT + NX, :] = pack.astype(bf16)
    sort_pair("gy", yn, ys, ya, yb)


def pack_z_kernel(tr, cu, after, zu, zd, t_s, c_s, sems):
    copies = [
        pltpu.make_async_copy(tr.at[:, pl.ds(0, 3)], t_s.at[0], sems.at[0]),
        pltpu.make_async_copy(cu.at[:, pl.ds(0, 2)], c_s.at[0], sems.at[1]),
        pltpu.make_async_copy(tr.at[:, pl.ds(NL - 3, 3)], t_s.at[1], sems.at[2]),
        pltpu.make_async_copy(cu.at[:, pl.ds(NL - 2, 2)], c_s.at[1], sems.at[3]),
    ]
    for copy in copies:
        copy.start()
    for copy in copies:
        copy.wait()
    for side, send in enumerate((zu, zd)):
        for c in range(2):
            for level in range(3):
                send[c * 3 + level] = t_s[side, c, level].astype(bf16)
            for level in range(2):
                send[6 + c * 2 + level] = c_s[side, c, level].astype(bf16)


def inside(axis, low):
    at = lax.axis_index(axis)
    return jnp.where(at > 0 if low else at < lax.axis_size(axis) - 1, 1.0, 0.0).astype(f32)


def field_pack(y):
    return y[YT : YT + NX, :].astype(f32)


def edge_packs(xw, xe):
    east, west = xw[XP : XP + 16, :].astype(f32), xe[XP : XP + 16, :].astype(f32)
    return [jnp.concatenate([east[4 * k : 4 * k + 4], west[4 * k : 4 * k + 4]], axis=0) for k in range(2)]


def pack_x_kernel(flux, ya_r, yb_r, table, tr, cu, xa, xb, yn_r, ys_r, xe, xw, rows_s, edge, sems):
    copies = []
    for k, source in enumerate((tr, cu)):
        copies.append(pltpu.make_async_copy(source.at[:, :, pl.ds(0, 8), :], edge.at[0, k], sems.at[2 * k]))
        copies.append(pltpu.make_async_copy(source.at[:, :, pl.ds(24, 8), :], edge.at[1, k], sems.at[2 * k + 1]))
    start(*copies)
    sort_pair("gy", ya_r, yb_r, ys_r, yn_r)
    packs = [field_pack(yn_r), field_pack(ys_r)]
    masks = [column(table[LAND + t : LAND + t + 1, 0:NX]) for t in range(NT)]
    in_south, in_north = inside("gy", True), inside("gy", False)
    for side, send in enumerate((xw, xe)):
        x = 0 if side == 0 else NX - 1
        first = 0 if side == 0 else NX - 4
        pack = jnp.concatenate([value[first : first + 4] for value in packs * 2], axis=0)
        send[XP : XP + 16, :] = pack.astype(bf16)
        for t in range(8):
            for f in range(4):
                if 2 <= t < 6:
                    block = flux[t - 2, f].astype(f32)
                else:
                    got, half = (yn_r, t) if t < 2 else (ys_r, t - 6)
                    at = YF + (half * 4 + f) * NX
                    block = got[at : at + NX, :].astype(f32) * (in_south if t < 2 else in_north)
                rows_s[t * 4 + f : t * 4 + f + 1, :] = block[x : x + 1]
        send[XF:XROWS, :] = rows_s[0:32, :].astype(bf16)
    wait(*copies)
    for side, send in enumerate((xw, xe)):
        rows = slice(0, 8) if side == 0 else slice(24, 32)
        for c in range(4):
            for plane in range(MASK_PLANE + 1):
                if plane == MASK_PLANE:
                    value = jnp.broadcast_to(masks[c][rows], (8, LANES))
                else:
                    kind, component, level = PLANES[plane]
                    value = edge[side, 0 if kind == "t" else 1, component, level, :, c * LANES : (c + 1) * LANES]
                first, count = x_rows(plane)
                keep = slice(0, count) if side == 0 else slice(8 - count, 8)
                rows_s[c * XPLANE + first : c * XPLANE + first + count, :] = value[keep]
        send[0:XP, :] = rows_s[...].astype(bf16)
    sort_pair("gx", xe, xw, xa, xb)


def remap_kernel(flux, yn_r, ys_r, table, w, after_x, part, wedge, rim, blk):
    zero = jnp.zeros((8, LANES), f32)
    in_south, in_north = inside("gy", True), inside("gy", False)
    for t in range(8):
        for f in range(4):
            if 2 <= t < 6:
                block = flux[t - 2, f].astype(f32)
            else:
                got, half = (yn_r, t) if t < 2 else (ys_r, t - 6)
                at = YF + (half * 4 + f) * NX
                block = got[at : at + NX, :].astype(f32) * (in_south if t < 2 else in_north)
            rim[t, f, 0:8, :] = zero
            rim[t, f, 8 : 8 + NX, :] = block
            rim[t, f, 8 + NX : 16 + NX, :] = zero

    def blocks(tile, row):
        code = jnp.broadcast_to(column(row), (NX, LANES))
        picked = [code == float(k) for k in range(9)]
        result = []
        for f in range(4):
            block = jnp.zeros((NX, LANES), f32)
            for k in range(9):
                x0 = 7 + k // 3
                block = jnp.where(picked[k], rim[tile + 2 + k % 3 - 1, f, x0 : x0 + NX, :], block)
            result.append(block)
        return result

    for t in range(NT):
        for s in range(2):
            row = 2 * t + s
            for f, block in enumerate(blocks(t, table[row : row + 1, 0:NX])):
                blk[row, f * NX : (f + 1) * NX, :] = block

    lane = lane_ids((NX, LANES))
    edges = [jnp.zeros((NX, LANES), f32) for f in range(4)]
    for got, tile, row, at in ((yn_r, -1, 6, 125), (ys_r, NT, 0, 0)):
        codes = got[YC : YC + 16, :].astype(f32)
        picked = [blocks(tile, codes[row + s : row + s + 1, 0:NX]) for s in range(2)]
        for d in range(3):
            weight = [
                got[YW + (d * 2 + s) * NX : YW + (d * 2 + s + 1) * NX, :].astype(f32) for s in range(2)
            ]
            for f in range(4):
                total = jnp.sum(weight[0] * picked[0][f] + weight[1] * picked[1][f], axis=1, keepdims=True)
                edges[f] = jnp.where(lane == at + d, total, edges[f])
    for f in range(4):
        part[4 * LANES + f * NX : 4 * LANES + (f + 1) * NX, :] = edges[f]

    for t in range(NT):

        def pair(i, _, t=t):
            x = 2 * i
            rows = [
                jnp.concatenate([blk[2 * t + s, pl.ds(x + j, 8, stride=NX), :] for j in range(2)], axis=0)
                for s in range(2)
            ]
            weights = jnp.concatenate(
                [jnp.concatenate([w[x + j, t, 0, s] for s in range(2)], axis=1) for j in range(2)], axis=0
            )
            product = lax.dot_general(
                jnp.concatenate(rows, axis=1).astype(bf16),
                weights,
                (((1,), (1,)), ((), ())),
                preferred_element_type=f32,
            )
            for j in range(2):
                block = product[8 * j : 8 * j + 4, j * LANES : (j + 1) * LANES]
                part[pl.ds(t * LANES + x + j, 4, stride=NX), :] = block
            return 0

        lax.fori_loop(0, NX // 2, pair, 0, unroll=8)
        for side, x in enumerate((0, NX - 1)):
            for s in range(2):
                wedge[side, t, s] = w[x, t, 0, s]


def rim_kernel(
    first_part, wedge, yn_r, ys_r, xa_r, xb_r, table, part, ua, ub, across, xe_r, xw_r, up, down, xs, rows_s
):
    sort_pair("gx", xa_r, xb_r, xw_r, xe_r)
    part[...] = first_part[...]
    near = [got[XF : XF + 32, :].astype(f32) * inside("gx", side == 0) for side, got in enumerate((xe_r, xw_r))]

    def blocks(side, tile, codes, row):
        x = 0 if side == 0 else NX - 1
        code = jnp.broadcast_to(codes[row : row + 1, x : x + 1], (4, LANES))
        block = jnp.zeros((4, LANES), f32)
        for k in range(3):
            at = (tile + 1 + k) * 4
            block = jnp.where(code == float(6 * side + k), near[side][at : at + 4], block)
        return block

    own_codes = table[...]
    gap = jnp.zeros((4, LANES), f32)
    for t in range(NT):
        rows = [
            jnp.concatenate([blocks(0, t, own_codes, 2 * t + s), gap, blocks(1, t, own_codes, 2 * t + s), gap], axis=0)
            for s in range(2)
        ]
        weights = jnp.concatenate(
            [jnp.concatenate([wedge[side, t, s] for s in range(2)], axis=1) for side in range(2)], axis=0
        )
        product = lax.dot_general(
            jnp.concatenate(rows, axis=1).astype(bf16), weights, (((1,), (1,)), ((), ())), preferred_element_type=f32
        )
        for side, x in enumerate((0, NX - 1)):
            part[pl.ds(t * LANES + x, 4, stride=NX), :] += product[8 * side : 8 * side + 4, side * LANES : (side + 1) * LANES]
    lane = lane_ids((4, LANES))
    for side, x in enumerate((0, NX - 1)):
        added = jnp.zeros((4, LANES), f32)
        for got, tile, row, at in ((yn_r, -1, 6, 125), (ys_r, NT, 0, 0)):
            codes = got[YC : YC + 16, :].astype(f32)
            picked = [blocks(side, tile, codes, row + s) for s in range(2)]
            for d in range(3):
                total = jnp.zeros((4, LANES), f32)
                for s in range(2):
                    first = YW + (d * 2 + s) * NX
                    weight = got[first : first + NX, :].astype(f32)[x : x + 1]
                    total += weight * picked[s]
                added = jnp.where(lane == at + d, jnp.sum(total, axis=1, keepdims=True), added)
        part[pl.ds(4 * LANES + x, 4, stride=NX), :] += added

    turned = part[4 * LANES : 5 * LANES, :].T
    halo = jnp.concatenate([turned[0:8], turned[LANES - 8 :]], axis=0).astype(bf16)
    own = part[0 : 4 * LANES, :].astype(bf16)
    for send in (up, down, across):
        send[0 : 4 * LANES, :] = own
        send[4 * LANES : CROWS, :] = halo
    xs[0] = xw_r[0:XP, :].astype(f32)
    xs[1] = xe_r[0:XP, :].astype(f32)
    south, north = edge_packs(xw_r, xe_r)
    low = lane_ids((8, LANES)) < 64
    for send, levels in ((up, (0, 1)), (down, (NL - 1, NL - 2))):
        for k, (kind, component, depth, column_at) in enumerate(FACE_ROWS):
            plane = PLANE_AT[(kind, component, levels[depth])]
            first, count = x_rows(plane)
            for c in range(4):
                for side in range(2):
                    at = c * XPLANE + first + (column_at if side == 0 else count - 1 - column_at)
                    to = c * 16 + side * 8 + k
                    rows_s[to : to + 1, :] = xs[side, at : at + 1, :]
            edge_col = jnp.where(low, unpack_north(north, plane), unpack_south(south, plane))
            for side in range(2):
                at = column_at if side == 0 else 7 - column_at
                to = 64 + side * 8 + k
                rows_s[to : to + 1, :] = edge_col[at : at + 1]
        send[CROWS:ZP, :] = rows_s[...].astype(bf16)
        pack, group = field_pack(ys_r), lane_ids((NX, LANES)) // 3
        moved = roll(field_pack(yn_r), 3 * APART, 1)
        for plane in sorted({PLANE_AT[(kind, component, levels[depth])] for kind, component, depth, _ in FACE_ROWS}):
            pack = jnp.where(group == plane + APART, moved, pack)
        send[ZP:ZROWS, :] = pack.astype(bf16)
    sort_pair("sec", down, up, ua, ub)


def flux_kernel(part, ua_r, ub_r, across_r, grid, ext, da, db, rows_s):
    got = [ref[4 * LANES : CROWS, :].astype(f32) for ref in (ua_r, ub_r, across_r)]
    turned = got[0] + got[1] + got[2]
    halo = jnp.concatenate([turned[0:8], jnp.zeros((LANES - 16, LANES), f32), turned[8:16]], axis=0).T
    for c in range(5):
        for f in range(4):
            at = c * LANES + f * NX
            total = part[at : at + NX, :]
            if c < 4:
                for ref in (ua_r, ub_r, across_r):
                    total = total + ref[at : at + NX, :].astype(f32)
            else:
                total = total + halo[f * NX : (f + 1) * NX]
            total = total * grid[MASK, c, OWN, :]
            ext[f, :, c * LANES : (c + 1) * LANES] = total
            rows_s[0, c * 16 + f * 4 : c * 16 + f * 4 + 4, :] = total[0:4]
            rows_s[1, c * 16 + f * 4 : c * 16 + f * 4 + 4, :] = total[NX - 4 : NX]
    first = jnp.where(even("gx"), 1, 0)
    da[...] = rows_s[first].astype(bf16)
    db[...] = rows_s[1 - first].astype(bf16)


def lane_next(value, lane):
    rolled = pltpu.roll(value, LANES - 1, 2)
    return jnp.where(lane == LANES - 1, jnp.concatenate([rolled[1:], rolled[:1]], axis=0), rolled)


def lane_prev(value, lane):
    rolled = pltpu.roll(value, 1, 2)
    return jnp.where(lane == 0, jnp.concatenate([rolled[-1:], rolled[:-1]], axis=0), rolled)


OWN, WEST, EAST = slice(12, 44), slice(8, 12), slice(44, 48)
PLANE = (5, 56, LANES)


MASK, BASE, VERT, KEPT = range(4)


def advance(here, above, below, velocity, grid, rows, open_below=None):
    r = rows.start
    lane = lane_ids((5, 8, LANES))

    def at(plane, c, where=rows):
        return plane[0][c, plane[1], :, where, :]

    base, vert, kept = (grid[k, :, rows, :] for k in (BASE, VERT, KEPT))
    if above is None:
        kept = kept + vert
    if open_below is not None:
        down = vert * open_below
        kept = kept + (vert - down)
    a, b = at(velocity, 0), at(velocity, 1)
    east, west, north, south = base - a, base + a, base - b, base + b
    results = []
    for c in range(2):
        g = at(here, c)
        new = kept * g
        new += east * at(here, c, slice(r + 1, r + 9)) + west * at(here, c, slice(r - 1, r + 7))
        new += north * lane_next(g, lane) + south * lane_prev(g, lane)
        if above is None:
            new += vert * at(below, c)
        elif open_below is None:
            new += vert * (at(above, c) + at(below, c))
        else:
            new += vert * at(above, c) + down * at(below, c)
        results.append(new)
    return results


def land_or(value, grid, rows, tr, c, level, x, out):
    for col in range(4):
        cells = slice(col * LANES, (col + 1) * LANES)
        out[:, cells] = jnp.where(grid[MASK, col, rows, :] > 0.0, value[col], tr[c, level, x : x + 8, cells])


def middle_kernel(
    tr, cu, yn_r, ys_r, xe_r, xw_r, table, after, after_zu, after_zd, g0, vel, g1, g2, grid, done, xs
):
    south, north = field_pack(yn_r), field_pack(ys_r)
    low = lane_ids((NX, LANES)) < 64
    edge_south, edge_north = edge_packs(xw_r, xe_r)
    edge_low = lane_ids((8, LANES)) < 64
    xs[0] = xw_r[0:XP, :].astype(f32)
    xs[1] = xe_r[0:XP, :].astype(f32)
    in_south, in_north, in_west, in_east = inside("gy", True), inside("gy", False), inside("gx", True), inside("gx", False)

    def pieces(plane, col, own):
        first, count = x_rows(plane)
        if col < 4:
            at = col * XPLANE + first
            east, west = xs[0, at : at + count, :], xs[1, at : at + count, :]
        else:
            own = jnp.where(low, unpack_north(north, plane), unpack_south(south, plane))
            edge = jnp.where(edge_low, unpack_north(edge_north, plane), unpack_south(edge_south, plane))
            east, west = edge[0:count], edge[8 - count : 8]
        return ((OWN, own), (slice(44, 44 + count), east), (slice(12 - count, 12), west))

    for col in range(5):
        own = None
        if col < 4:
            own = jnp.broadcast_to(column(table[LAND + col : LAND + col + 1, 0:NX]), (NX, LANES))
        for (rows, value), in_x in zip(pieces(MASK_PLANE, col, own), (1.0, in_east, in_west)):
            if col == 4:
                value = value * jnp.where(low[0 : value.shape[0]], in_north, in_south)
            grid[MASK, col, rows, :] = value * in_x
    lane = lane_ids((5, 8, LANES))
    for r in range(8, 48, 8):
        rows, m = slice(r, r + 8), grid[MASK, :, r : r + 8, :]
        around = grid[MASK, :, r + 1 : r + 9, :] + grid[MASK, :, r - 1 : r + 7, :] + lane_next(m, lane) + lane_prev(m, lane)
        grid[BASE, :, rows, :] = DIFFUSION * m
        grid[VERT, :, rows, :] = VERTICAL * m
        grid[KEPT, :, rows, :] = m * (1.0 - 2.0 * VERTICAL - DIFFUSION * around)

    for col in range(5):
        for plane, (kind, c, level) in enumerate(PLANES):
            source, target = (tr, g0) if kind == "t" else (cu, vel)
            own = source[c, level, :, col * LANES : (col + 1) * LANES] if col < 4 else None
            for rows, value in pieces(plane, col, own):
                scale = grid[MASK, col, rows, :]
                target[c, level, col, rows, :] = value * (scale if kind == "t" else ADVECTION * scale)

    def sweep(src, src_at, dst, dst_at, levels):
        def one_level(l, _):
            for r in range(8, 48, 8):
                rows = slice(r, r + 8)
                at = l - src_at
                step = advance((src, at), (src, at - 1), (src, at + 1), (vel, l - 3), grid, rows)
                for c, value in enumerate(step):
                    dst[c, l - dst_at, :, rows, :] = value
            return 0

        lax.fori_loop(levels[0], levels[1], one_level, 0, unroll=2)

    sweep(g0, 3, g1, 4, (4, 12))
    sweep(g1, 4, g2, 5, (5, 11))

    def last(l, _):
        for r in range(12, 44, 8):
            rows = slice(r, r + 8)
            at = l - 5
            step = advance((g2, at), (g2, at - 1), (g2, at + 1), (vel, l - 3), grid, rows)
            for c, value in enumerate(step):
                land_or(value, grid, rows, tr, c, l - 3, r - 12, done.at[c, l - 6, r - 12 : r - 4])
        return 0

    lax.fori_loop(6, 10, last, 0, unroll=2)


def face_steps(planes, velocities, levels, out, grid, tr, starts, last_starts, out_x=lambda x: x, open_below=None):
    for k in range(3):
        for l in levels[k]:
            here, above, below = (planes[k].get(i) for i in (l, l - 1, l + 1))
            floor = open_below if l == 12 else None
            for r in starts if k < 2 else last_starts:
                rows = slice(r, r + 8)
                step = advance(here, above, below, velocities[l], grid, rows, floor)
                for c, value in enumerate(step):
                    if k < 2:
                        ref, index = planes[k + 1][l]
                        ref[c, index, :, rows, :] = value
                    else:
                        x = r - 12
                        land_or(value, grid, rows, tr, c, l - 3, x, out.at[c, l - levels[2][0], out_x(x) : out_x(x) + 8])


def planes_of(*runs):
    return {first + k: (ref, index + k) for first, count, ref, index in runs for k in range(count)}


def forced(velocities, tracers):
    return (
        (velocities, 0, ADVECTION * WIND_GAIN),
        (velocities, 1, ADVECTION * WIND_GAIN),
        (tracers, 0, HEAT_GAIN),
        (tracers, 1, -SALT_GAIN),
    )


WHOLE, INNER = range(8, 48, 8), range(12, 44, 8)


def outer_kernel(
    tr, g0, vel, g1, g2, grid, zu_r, zd_r, ua_r, ub_r, ext, middle, after, out, ocean_flux, s0, sv, s1, s2,
    up_r, down_r, b0, bv, b1, b2, top, bottom, sems,
):
    sec = lax.axis_index("sec")
    writes = [
        pltpu.make_async_copy(ext.at[:, :, pl.ds(0, 512)], ocean_flux, sems.at[0]),
        pltpu.make_async_copy(middle.at[:, pl.ds(1, 3)], out.at[:, pl.ds(4, 3)], sems.at[1]),
        pltpu.make_async_copy(bottom, out.at[:, pl.ds(7, 3)], sems.at[2]),
    ]
    start(*writes[:2])
    sort_pair("sec", ua_r.at[pl.ds(CROWS, ZROWS - CROWS)], ub_r.at[pl.ds(CROWS, ZROWS - CROWS)], up_r, down_r)
    low = lane_ids((NX, LANES)) < 64

    def halo_planes(got, z, face, tracers, velocities):
        pack = got[ZP - CROWS : ZROWS - CROWS, :].astype(f32)
        near = [got[c * 16 : (c + 1) * 16, :].astype(f32) for c in range(5)]

        def put(target, body, plane, at, scale):
            for col in range(4):
                value = body[:, col * LANES : (col + 1) * LANES].astype(f32)
                target[col, OWN, :] = value * (scale * grid[MASK, col, OWN, :])
            if plane is None:
                return
            col4 = jnp.where(low, unpack_north(pack, plane), unpack_south(pack, plane + APART))
            target[4, OWN, :] = col4 * (scale * grid[MASK, 4, OWN, :])
            for col in range(5):
                for k, row in enumerate(at):
                    for to, value in ((44 + k, near[col][row : row + 1]), (11 - k, near[col][8 + row : 9 + row])):
                        target[col, to : to + 1, :] = value * (scale * grid[MASK, col, to : to + 1, :])

        for c in range(2):
            for k in range(3):
                depth = k if face == 1 else 2 - k
                level = k if face == 1 else 7 + k
                plane = PLANE_AT[("t", c, level)] if depth < 2 else None
                at = (3 * c, 3 * c + 1) if depth == 0 else (3 * c + 2,)
                put(tracers.at[c, k], z[c * 3 + k], plane, at, 1.0)
            for k in range(2):
                depth = k if face == 1 else 1 - k
                plane = PLANE_AT[("c", c, 0 if face == 1 else 9)] if depth == 0 else None
                put(velocities.at[c, k], z[6 + c * 2 + k], plane, (6 + c,), ADVECTION)

    halo_planes(up_r, zu_r, 1, b0, bv)
    face_steps(
        (
            planes_of((11, 2, g0, 8), (13, 3, b0, 0)),
            planes_of((10, 2, g1, 6), (12, 3, b1, 0)),
            planes_of((9, 2, g2, 4), (11, 3, b2, 0)),
        ),
        planes_of((10, 3, vel, 7), (13, 2, bv, 0)),
        (range(12, 15), range(11, 14), range(10, 13)),
        bottom, grid, tr, WHOLE, INNER,
        open_below=jnp.where(sec < lax.axis_size("sec") - 1, 1.0, 0.0).astype(f32),
    )
    writes[2].start()

    @pl.when(sec != 0)
    def _():
        level3 = pltpu.make_async_copy(middle.at[:, pl.ds(0, 1)], out.at[:, pl.ds(3, 1)], sems.at[3])
        level3.start()
        halo_planes(down_r, zd_r, 0, s0, sv)
        face_steps(
            (
                planes_of((0, 3, s0, 0), (3, 2, g0, 0)),
                planes_of((1, 3, s1, 0), (4, 2, g1, 0)),
                planes_of((2, 3, s2, 0), (5, 2, g2, 0)),
            ),
            planes_of((1, 2, sv, 0), (3, 3, vel, 0)),
            (range(1, 4), range(2, 5), range(3, 6)),
            top, grid, tr, WHOLE, INNER,
        )
        write = pltpu.make_async_copy(top.at[:, pl.ds(0, 3)], out.at[:, pl.ds(0, 3)], sems.at[4])
        write.start()
        wait(level3, write)

    @pl.when(sec == 0)
    def _():
        for f, (ref, c, gain) in enumerate(forced(sv, s0)):
            source = vel if f < 2 else g0
            for col in range(5):
                for r in range(8, 48, 8):
                    ref[c, 0, col, r : r + 8, :] = source[c, 0, col, r : r + 8, :]
                ref[c, 0, col, OWN, :] += gain * ext[f, :, col * LANES : (col + 1) * LANES] * grid[MASK, col, OWN, :]
        face_steps(
            surface_planes(s0, s1, s2, g0, g1, g2),
            planes_of((3, 1, sv, 0), (4, 3, vel, 1)),
            SURFACE_LEVELS,
            top, grid, tr, WHOLE, INNER,
        )
        write = pltpu.make_async_copy(top, out.at[:, pl.ds(0, 4)], sems.at[3])
        write.start()
        write.wait()

    wait(*writes)


SURFACE_LEVELS = (range(3, 5), range(3, 6), range(3, 7))


def surface_planes(s0, s1, s2, g0, g1, g2):
    return (
        planes_of((3, 1, s0, 0), (4, 2, g0, 1)),
        planes_of((3, 2, s1, 0), (5, 2, g1, 1)),
        planes_of((3, 3, s2, 0), (6, 2, g2, 1)),
    )


def surface_kernel(
    unfinished, tr, s0, sv, s1, s2, g0, vel, g1, g2, grid, da_r, db_r, out, e0, ev, e1, e2, edge, sems
):
    @pl.when(lax.axis_index("sec") == 0)
    def _():
        got_a, got_b = da_r[...].astype(f32), db_r[...].astype(f32)
        halo = (jnp.where(even("gx"), got_b, got_a), jnp.where(even("gx"), got_a, got_b))
        for c in range(2):
            for target, source, planes, groups in (
                (e0, s0, 1, (8, 16, 32, 40)),
                (ev, sv, 1, (8, 16, 32, 40)),
                (e1, s1, 2, (16, 32)),
                (e2, s2, 3, (16, 32)),
            ):
                for k in range(planes):
                    for r in groups:
                        target[c, k, :, r : r + 8, :] = source[c, k, :, r : r + 8, :]
        for side, rows in enumerate((WEST, EAST)):
            for f, (ref, c, gain) in enumerate(forced(ev, e0)):
                for col in range(5):
                    r = col * 16 + f * 4
                    ref[c, 0, col, rows, :] += gain * halo[side][r : r + 4] * grid[MASK, col, rows, :]
        face_steps(
            surface_planes(e0, e1, e2, g0, g1, g2),
            planes_of((3, 1, ev, 0), (4, 3, vel, 1)),
            SURFACE_LEVELS,
            edge, grid, tr, (8, 40), (12, 36), lambda x: 0 if x == 0 else 8,
        )
        writes = [
            pltpu.make_async_copy(
                edge.at[:, :, pl.ds(8 * side, 8)], out.at[:, pl.ds(0, 4), pl.ds(24 * side, 8)], sems.at[side]
            )
            for side in range(2)
        ]
        start(*writes)
        wait(*writes)


ANY = pl.BlockSpec(memory_space=pl.ANY)
HBM = pl.BlockSpec(memory_space=pltpu.HBM)
VMEM = pl.BlockSpec(memory_space=pltpu.VMEM)


def hbm(value):
    return pltpu.with_memory_space_constraint(value, pltpu.HBM)


def call(kernel, in_specs, outs, scratch, name, bytes_accessed, out_specs=None, aliases=None):
    return pl.pallas_call(
        kernel,
        out_shape=[jax.ShapeDtypeStruct(shape, dtype) for shape, dtype in outs],
        in_specs=in_specs,
        out_specs=out_specs or [VMEM] * len(outs),
        scratch_shapes=scratch,
        input_output_aliases=aliases or {},
        compiler_params=pltpu.CompilerParams(vmem_limit_bytes=VMEM_BYTES),
        cost_estimate=pl.CostEstimate(flops=0, bytes_accessed=bytes_accessed, transcendentals=0),
        name=name,
    )


def shifted(value, axis, step):
    count = lax.axis_size(axis)
    return lax.ppermute(value, axis, [(i, (i + step) % count) for i in range(count)])


def swapped(a, b, axis):
    count = lax.axis_size(axis)
    one = [(i, i ^ 1) for i in range(count)]
    other = [(i, (i + (1 if i % 2 else -1)) % count) for i in range(count)]
    return lax.ppermute(a, axis, one), lax.ppermute(b, axis, other)


def on_device(air_surface, remap_weights, sources, live_count, land_sea, tracers, currents):
    src = hbm(jnp.transpose(sources[:, :, 0, :], (1, 2, 0)))
    live = hbm(jnp.transpose(live_count, (1, 2, 0)))
    land = hbm(jnp.transpose(land_sea, (1, 0)))
    dma = pltpu.SemaphoreType.DMA

    ya, yb, flux, table = call(
        pack_y_kernel,
        [HBM] * 7,
        [((YROWS, LANES), bf16), ((YROWS, LANES), bf16), ((NT, 4, NX, LANES), bf16), ((16, LANES), f32)],
        [
            pltpu.VMEM((YROWS, LANES), bf16),
            pltpu.VMEM((YROWS, LANES), bf16),
            pltpu.VMEM((NT, 2, NX), jnp.int32),
            pltpu.VMEM((NT, 1, NX), jnp.int32),
            pltpu.VMEM((NT, NX), jnp.int32),
            pltpu.VMEM((5, NX * NT, LANES), f32),
            pltpu.VMEM((NX, 2, 16, LANES), bf16),
            pltpu.VMEM((NX, 2, 16, LANES), bf16),
            pltpu.VMEM((192, LANES), f32),
            pltpu.VMEM((2, 2, 2, NL, NX, LANES), f32),
            dma((10,)),
        ],
        "pack_y",
        6_000_000,
    )(hbm(air_surface.reshape(5, NX * NT, LANES)), src, live, land, hbm(remap_weights), hbm(tracers), hbm(currents))
    ya_r, yb_r = swapped(ya, yb, "gy")

    zu, zd = call(
        pack_z_kernel,
        [ANY, ANY, ANY],
        [((10, NX, 512), bf16)] * 2,
        [pltpu.VMEM((2, 2, 3, NX, 512), f32), pltpu.VMEM((2, 2, 2, NX, 512), f32), dma((4,))],
        "pack_z",
        3_000_000,
    )(tracers, currents, table)
    zu_r = shifted(zu, "sec", -1)
    zd_r = shifted(zd, "sec", 1)

    xa, xb, yn_r, ys_r = call(
        pack_x_kernel,
        [VMEM, VMEM, VMEM, VMEM, ANY, ANY],
        [((XROWS, LANES), bf16)] * 2 + [((YROWS, LANES), bf16)] * 2,
        [pltpu.VMEM((XROWS, LANES), bf16)] * 2
        + [pltpu.VMEM((XP, LANES), f32), pltpu.VMEM((2, 2, 2, NL, 8, 512), f32), dma((4,))],
        "pack_x",
        3_000_000,
    )(flux, ya_r, yb_r, table, tracers, currents)
    xa_r, xb_r = swapped(xa, xb, "gx")

    first_part, wedge = call(
        remap_kernel,
        [VMEM] * 5 + [ANY],
        [((5 * LANES, LANES), f32), ((2, NT, 2, LANES, LANES), bf16)],
        [
            pltpu.VMEM((8, 4, 48, LANES), f32),
            pltpu.VMEM((2 * NT, 2 * LANES, LANES), f32),
        ],
        "remap",
        18_000_000,
    )(flux, yn_r, ys_r, table, remap_weights, xa)
    part, ua, ub, across, xe_r, xw_r = call(
        rim_kernel,
        [VMEM] * 7,
        [((5 * LANES, LANES), f32)]
        + [((rows, LANES), bf16) for rows in (ZROWS, ZROWS, CROWS, XROWS, XROWS)],
        [pltpu.VMEM((ZROWS, LANES), bf16)] * 2 + [pltpu.VMEM((2, XP, LANES), f32), pltpu.VMEM((80, LANES), f32)],
        "rim",
        4_000_000,
    )(first_part, wedge, yn_r, ys_r, xa_r, xb_r, table)
    across_r = shifted(across, "sec", 2)
    ua_r, ub_r = swapped(ua, ub, "sec")

    plane = (5, 56, LANES)
    g0, vel, g1, g2, grid, middle = call(
        middle_kernel,
        [VMEM] * 7 + [ANY] * 3,
        [
            ((2, NL) + plane, f32),
            ((2, NL) + plane, f32),
            ((2, NL - 2) + plane, f32),
            ((2, NL - 4) + plane, f32),
            ((4,) + plane, f32),
            ((2, NL - 6, NX, 512), f32),
        ],
        [
            pltpu.VMEM((2, XP, LANES), f32),
        ],
        "middle",
        20_000_000,
    )(tracers, currents, yn_r, ys_r, xe_r, xw_r, table, across, zu_r, zd_r)

    ext, da, db = call(
        flux_kernel,
        [VMEM] * 5,
        [((4, NX, 5 * LANES), f32), ((80, LANES), bf16), ((80, LANES), bf16)],
        [pltpu.VMEM((2, 80, LANES), f32)],
        "flux_sum",
        3_000_000,
    )(part, ua_r, ub_r, across_r, grid)
    da_r, db_r = swapped(da, db, "gx")

    unfinished, ocean_flux, s0, sv, s1, s2 = call(
        outer_kernel,
        [VMEM] * 12 + [ANY],
        [((2, NL, NX, 512), f32), ((4, NX, 512), f32)] + [((2, count) + plane, f32) for count in (3, 2, 3, 3)],
        [pltpu.VMEM((ZROWS - CROWS, LANES), bf16)] * 2
        + [pltpu.VMEM((2, count) + plane, f32) for count in (3, 2, 3, 3)]
        + [pltpu.VMEM((2, 4, NX, 512), f32), pltpu.VMEM((2, 3, NX, 512), f32), dma((5,))],
        "outer",
        18_000_000,
        [HBM, HBM] + [VMEM] * 4,
    )(tracers, g0, vel, g1, g2, grid, zu_r, zd_r, ua_r, ub_r, ext, middle, da)

    (tracers_out,) = call(
        surface_kernel,
        [HBM] + [VMEM] * 12,
        [((2, NL, NX, 512), f32)],
        [pltpu.VMEM((2, count) + plane, f32) for count in (1, 1, 2, 3)]
        + [pltpu.VMEM((2, 4, 16, 512), f32), dma((2,))],
        "surface",
        8_000_000,
        [HBM],
        {0: 0},
    )(unfinished, tracers, s0, sv, s1, s2, g0, vel, g1, g2, grid, da_r, db_r)
    return (tracers_out, ocean_flux)


def solution(mesh):
    return jax.shard_map(
        on_device,
        mesh=mesh,
        in_specs=(
            P(None, "gx", "gy", "sec", None),
            P("gx", "gy", "sec", None, None, None),
            P("gx", "gy", "sec", None),
            P("gx", "gy", "sec"),
            P("gx", "gy"),
            P(None, "sec", "gx", "gy"),
            P(None, "sec", "gx", "gy"),
        ),
        out_specs=(P(None, "sec", "gx", "gy"), P(None, "gx", "gy")),
        check_vma=False,
    )
```

```python
import jax
import jax.numpy as jnp
from jax import lax
from jax.experimental import pallas as pl
from jax.experimental.pallas import tpu as pltpu
from jax.sharding import PartitionSpec as P

f32 = jnp.float32
bf16 = jnp.bfloat16

DRAG = 0.6
WIND_GAIN = 0.5
HEAT_GAIN = 0.5
SALT_GAIN = 0.5
DIFFUSION = 0.15
ADVECTION = 0.5
VERTICAL = 0.2

NX = 32
NT = 4
NL = 10
LANES = 128

YF, YW, YC, YT, YROWS = 0, 256, 448, 464, 496
XPLANE, XP, XF, XROWS = 112, 448, 464, 496
CROWS, ZP, ZROWS = 528, 608, 640
LAND = 8

VMEM_BYTES = 24 * 1024 * 1024

PLANES = (
    [("t", 0, level) for level in range(NL)]
    + [("t", 1, level) for level in range(NL)]
    + [("c", 0, 0), ("c", 0, 9), ("c", 1, 0), ("c", 1, 9)]
    + [("c", 0, level) for level in range(1, 9)]
    + [("c", 1, level) for level in range(1, 9)]
)
MASK_PLANE = len(PLANES)
PLANE_AT = {plane: index for index, plane in enumerate(PLANES)}


def x_rows(plane):
    if plane < 20:
        return 3 * plane, 3
    if plane < MASK_PLANE:
        return 60 + 2 * (plane - 20), 2
    return 100, 3


FACE_ROWS = (
    ("t", 0, 0, 0), ("t", 0, 0, 1), ("t", 0, 1, 0),
    ("t", 1, 0, 0), ("t", 1, 0, 1), ("t", 1, 1, 0),
    ("c", 0, 0, 0), ("c", 1, 0, 0),
)
APART = 6


def column(row):
    rows = lax.broadcasted_iota(jnp.int32, (NX, NX), 0)
    cols = lax.broadcasted_iota(jnp.int32, (NX, NX), 1)
    return jnp.sum(jnp.where(rows == cols, jnp.broadcast_to(row, (NX, NX)), 0.0), axis=1, keepdims=True)


def lane_ids(shape):
    return lax.broadcasted_iota(jnp.int32, shape, len(shape) - 1)


def start(*copies):
    for copy in copies:
        copy.start()


def wait(*copies):
    for copy in copies:
        copy.wait()


def even(axis):
    return lax.axis_index(axis) % 2 == 0


def sort_pair(axis, a, b, plus, minus):
    @pl.when(even(axis))
    def _():
        plus[...] = a[...]
        minus[...] = b[...]

    @pl.when(jnp.logical_not(even(axis)))
    def _():
        plus[...] = b[...]
        minus[...] = a[...]


def roll(value, shift, axis):
    shift %= value.shape[axis]
    return value if shift == 0 else pltpu.roll(value, shift, axis)


def unpack_north(pack, plane, rows=slice(None)):
    return roll(pack[rows], -3 * plane, 1)


def unpack_south(pack, plane, rows=slice(None)):
    return roll(pack[rows], 125 - 3 * plane, 1)


def pack_y_kernel(
    air, src_h, live_h, land_h, w, tr, cu, ya, yb, flux, table, yn, ys, src, live, land, air_s, wn, ws, rows_s, edge, sems
):
    copies = [pltpu.make_async_copy(air, air_s, sems.at[0])]
    copies.append(pltpu.make_async_copy(w.at[:, NT - 1, 0, :, pl.ds(112, 16), :], wn, sems.at[1]))
    copies.append(pltpu.make_async_copy(w.at[:, 0, 0, :, pl.ds(0, 16), :], ws, sems.at[2]))
    for k, source in enumerate((tr, cu)):
        copies.append(pltpu.make_async_copy(source.at[:, :, :, pl.ds(384, 128)], edge.at[0, k], sems.at[3 + k]))
        copies.append(pltpu.make_async_copy(source.at[:, :, :, pl.ds(0, 128)], edge.at[1, k], sems.at[5 + k]))
    small = [
        pltpu.make_async_copy(source, target, sems.at[7 + k])
        for k, (source, target) in enumerate(((src_h, src), (live_h, live), (land_h, land)))
    ]
    start(copies[0], *small, *copies[1:])
    copies[0].wait()
    for t in range(NT):
        u, v, ta, qa, ts = (air_s[k, pl.ds(t, NX, stride=NT), :] for k in range(5))
        rate = DRAG * (1.0 + 0.5 * jnp.tanh(ts - ta)) * jnp.sqrt(u * u + v * v + 1.0)
        values = (rate * u, rate * v, rate * (ts - ta), rate * (jnp.exp(0.3 * ts) - qa))
        for f, value in enumerate(values):
            value = value.astype(bf16)
            flux[t, f] = value
            at = YF + ((t % 2) * 4 + f) * NX
            (ys if t < 2 else yn)[at : at + NX, :] = value
    wait(*small)
    slot = lax.broadcasted_iota(jnp.int32, (NT, 2, NX), 1)
    codes = jnp.where(slot < live[...], src[...], 9).astype(f32)
    table[...] = jnp.zeros((16, LANES), f32)
    for t in range(NT):
        table[2 * t : 2 * t + 2, 0:NX] = codes[t]
    table[LAND : LAND + NT, 0:NX] = land[...].astype(f32)
    sent = table[...].astype(bf16)
    yn[YC : YC + 16, :] = sent
    ys[YC : YC + 16, :] = sent
    wait(*copies[1:3])
    for send, tile, first in ((yn, wn, 13), (ys, ws, 0)):
        for x in range(NX):
            for s in range(2):
                block = tile[x, s].astype(f32)
                for d in range(3):
                    rows_s[pl.ds(d * 64 + s * 32 + x, 1), :] = block[first + d : first + d + 1]
        send[YW : YW + 192, :] = rows_s[...].astype(bf16)
    group = lane_ids((NX, LANES)) // 3
    packs = [jnp.zeros((NX, LANES), f32)] * 2
    for plane in range(MASK_PLANE + 1):
        if plane == 0:
            wait(copies[3], copies[4])
        if plane == 20:
            wait(copies[5], copies[6])
        for side in range(2):
            if plane == MASK_PLANE:
                tile = LAND + (NT - 1 if side == 0 else 0)
                value = jnp.broadcast_to(column(table[tile : tile + 1, 0:NX]), (NX, LANES))
            else:
                kind, c, level = PLANES[plane]
                value = edge[side, 0 if kind == "t" else 1, c, level]
            turn = 3 * plane - (125 if side == 0 else 0)
            packs[side] = jnp.where(group == plane, roll(value, turn, 1), packs[side])
    for send, pack in zip((yn, ys), packs):
        send[YT : YT + NX, :] = pack.astype(bf16)
    sort_pair("gy", yn, ys, ya, yb)


def pack_z_kernel(tr, cu, after, zu, zd, t_s, c_s, sems):
    copies = [
        pltpu.make_async_copy(tr.at[:, pl.ds(0, 3)], t_s.at[0], sems.at[0]),
        pltpu.make_async_copy(cu.at[:, pl.ds(0, 2)], c_s.at[0], sems.at[1]),
        pltpu.make_async_copy(tr.at[:, pl.ds(NL - 3, 3)], t_s.at[1], sems.at[2]),
        pltpu.make_async_copy(cu.at[:, pl.ds(NL - 2, 2)], c_s.at[1], sems.at[3]),
    ]
    for copy in copies:
        copy.start()
    for copy in copies:
        copy.wait()
    for side, send in enumerate((zu, zd)):
        for c in range(2):
            for level in range(3):
                send[c * 3 + level] = t_s[side, c, level].astype(bf16)
            for level in range(2):
                send[6 + c * 2 + level] = c_s[side, c, level].astype(bf16)


def inside(axis, low):
    at = lax.axis_index(axis)
    return jnp.where(at > 0 if low else at < lax.axis_size(axis) - 1, 1.0, 0.0).astype(f32)


def field_pack(y):
    return y[YT : YT + NX, :].astype(f32)


def edge_packs(xw, xe):
    east, west = xw[XP : XP + 16, :].astype(f32), xe[XP : XP + 16, :].astype(f32)
    return [jnp.concatenate([east[4 * k : 4 * k + 4], west[4 * k : 4 * k + 4]], axis=0) for k in range(2)]


def pack_x_kernel(flux, yb_r, ya_r, table, tr, cu, xa, xb, yn_r, ys_r, xe, xw, rows_s, edge, sems):
    copies = []
    for k, source in enumerate((tr, cu)):
        copies.append(pltpu.make_async_copy(source.at[:, :, pl.ds(0, 8), :], edge.at[0, k], sems.at[2 * k]))
        copies.append(pltpu.make_async_copy(source.at[:, :, pl.ds(24, 8), :], edge.at[1, k], sems.at[2 * k + 1]))
    start(*copies)
    sort_pair("gy", ya_r, yb_r, ys_r, yn_r)
    packs = [field_pack(yn_r), field_pack(ys_r)]
    masks = [column(table[LAND + t : LAND + t + 1, 0:NX]) for t in range(NT)]
    in_south, in_north = inside("gy", True), inside("gy", False)
    for side, send in enumerate((xw, xe)):
        x = 0 if side == 0 else NX - 1
        first = 0 if side == 0 else NX - 4
        pack = jnp.concatenate([value[first : first + 4] for value in packs * 2], axis=0)
        send[XP : XP + 16, :] = pack.astype(bf16)
        for t in range(8):
            for f in range(4):
                if 2 <= t < 6:
                    block = flux[t - 2, f].astype(f32)
                else:
                    got, half = (yn_r, t) if t < 2 else (ys_r, t - 6)
                    at = YF + (half * 4 + f) * NX
                    block = got[at : at + NX, :].astype(f32) * (in_south if t < 2 else in_north)
                rows_s[t * 4 + f : t * 4 + f + 1, :] = block[x : x + 1]
        send[XF:XROWS, :] = rows_s[0:32, :].astype(bf16)
    wait(*copies)
    for side, send in enumerate((xw, xe)):
        rows = slice(0, 8) if side == 0 else slice(24, 32)
        for c in range(4):
            for plane in range(MASK_PLANE + 1):
                if plane == MASK_PLANE:
                    value = jnp.broadcast_to(masks[c][rows], (8, LANES))
                else:
                    kind, component, level = PLANES[plane]
                    value = edge[side, 0 if kind == "t" else 1, component, level, :, c * LANES : (c + 1) * LANES]
                first, count = x_rows(plane)
                keep = slice(0, count) if side == 0 else slice(8 - count, 8)
                rows_s[c * XPLANE + first : c * XPLANE + first + count, :] = value[keep]
        send[0:XP, :] = rows_s[...].astype(bf16)
    sort_pair("gx", xe, xw, xa, xb)


def remap_kernel(flux, yn_r, ys_r, table, w, after_x, part, wedge, rim, blk):
    zero = jnp.zeros((8, LANES), f32)
    in_south, in_north = inside("gy", True), inside("gy", False)
    for t in range(8):
        for f in range(4):
            if 2 <= t < 6:
                block = flux[t - 2, f].astype(f32)
            else:
                got, half = (yn_r, t) if t < 2 else (ys_r, t - 6)
                at = YF + (half * 4 + f) * NX
                block = got[at : at + NX, :].astype(f32) * (in_south if t < 2 else in_north)
            rim[t, f, 0:8, :] = zero
            rim[t, f, 8 : 8 + NX, :] = block
            rim[t, f, 8 + NX : 16 + NX, :] = zero

    def blocks(tile, row):
        code = jnp.broadcast_to(column(row), (NX, LANES))
        picked = [code == float(k) for k in range(9)]
        result = []
        for f in range(4):
            block = jnp.zeros((NX, LANES), f32)
            for k in range(9):
                x0 = 7 + k // 3
                block = jnp.where(picked[k], rim[tile + 2 + k % 3 - 1, f, x0 : x0 + NX, :], block)
            result.append(block)
        return result

    for t in range(NT):
        for s in range(2):
            row = 2 * t + s
            for f, block in enumerate(blocks(t, table[row : row + 1, 0:NX])):
                blk[row, f * NX : (f + 1) * NX, :] = block

    lane = lane_ids((NX, LANES))
    edges = [jnp.zeros((NX, LANES), f32) for f in range(4)]
    for got, tile, row, at in ((yn_r, -1, 6, 125), (ys_r, NT, 0, 0)):
        codes = got[YC : YC + 16, :].astype(f32)
        picked = [blocks(tile, codes[row + s : row + s + 1, 0:NX]) for s in range(2)]
        for d in range(3):
            weight = [
                got[YW + (d * 2 + s) * NX : YW + (d * 2 + s + 1) * NX, :].astype(f32) for s in range(2)
            ]
            for f in range(4):
                total = jnp.sum(weight[0] * picked[0][f] + weight[1] * picked[1][f], axis=1, keepdims=True)
                edges[f] = jnp.where(lane == at + d, total, edges[f])
    for f in range(4):
        part[4 * LANES + f * NX : 4 * LANES + (f + 1) * NX, :] = edges[f]

    for t in range(NT):

        def pair(i, _, t=t):
            x = 2 * i
            rows = [
                jnp.concatenate([blk[2 * t + s, pl.ds(x + j, 8, stride=NX), :] for j in range(2)], axis=0)
                for s in range(2)
            ]
            weights = jnp.concatenate(
                [jnp.concatenate([w[x + j, t, 0, s] for s in range(2)], axis=1) for j in range(2)], axis=0
            )
            product = lax.dot_general(
                jnp.concatenate(rows, axis=1).astype(bf16),
                weights,
                (((1,), (1,)), ((), ())),
                preferred_element_type=f32,
            )
            for j in range(2):
                block = product[8 * j : 8 * j + 4, j * LANES : (j + 1) * LANES]
                part[pl.ds(t * LANES + x + j, 4, stride=NX), :] = block
            return 0

        lax.fori_loop(0, NX // 2, pair, 0, unroll=8)
        for side, x in enumerate((0, NX - 1)):
            for s in range(2):
                wedge[side, t, s] = w[x, t, 0, s]


def rim_kernel(
    first_part, wedge, yn_r, ys_r, xb_r, xa_r, table, part, ua, ub, across, xe_r, xw_r, up, down, xs, rows_s
):
    sort_pair("gx", xa_r, xb_r, xw_r, xe_r)
    part[...] = first_part[...]
    near = [got[XF : XF + 32, :].astype(f32) * inside("gx", side == 0) for side, got in enumerate((xe_r, xw_r))]

    def blocks(side, tile, codes, row):
        x = 0 if side == 0 else NX - 1
        code = jnp.broadcast_to(codes[row : row + 1, x : x + 1], (4, LANES))
        block = jnp.zeros((4, LANES), f32)
        for k in range(3):
            at = (tile + 1 + k) * 4
            block = jnp.where(code == float(6 * side + k), near[side][at : at + 4], block)
        return block

    own_codes = table[...]
    gap = jnp.zeros((4, LANES), f32)
    for t in range(NT):
        rows = [
            jnp.concatenate([blocks(0, t, own_codes, 2 * t + s), gap, blocks(1, t, own_codes, 2 * t + s), gap], axis=0)
            for s in range(2)
        ]
        weights = jnp.concatenate(
            [jnp.concatenate([wedge[side, t, s] for s in range(2)], axis=1) for side in range(2)], axis=0
        )
        product = lax.dot_general(
            jnp.concatenate(rows, axis=1).astype(bf16), weights, (((1,), (1,)), ((), ())), preferred_element_type=f32
        )
        for side, x in enumerate((0, NX - 1)):
            part[pl.ds(t * LANES + x, 4, stride=NX), :] += product[8 * side : 8 * side + 4, side * LANES : (side + 1) * LANES]
    lane = lane_ids((4, LANES))
    for side, x in enumerate((0, NX - 1)):
        added = jnp.zeros((4, LANES), f32)
        for got, tile, row, at in ((yn_r, -1, 6, 125), (ys_r, NT, 0, 0)):
            codes = got[YC : YC + 16, :].astype(f32)
            picked = [blocks(side, tile, codes, row + s) for s in range(2)]
            for d in range(3):
                total = jnp.zeros((4, LANES), f32)
                for s in range(2):
                    first = YW + (d * 2 + s) * NX
                    weight = got[first : first + NX, :].astype(f32)[x : x + 1]
                    total += weight * picked[s]
                added = jnp.where(lane == at + d, jnp.sum(total, axis=1, keepdims=True), added)
        part[pl.ds(4 * LANES + x, 4, stride=NX), :] += added

    turned = part[4 * LANES : 5 * LANES, :].T
    halo = jnp.concatenate([turned[0:8], turned[LANES - 8 :]], axis=0).astype(bf16)
    own = part[0 : 4 * LANES, :].astype(bf16)
    for send in (up, down, across):
        send[0 : 4 * LANES, :] = own
        send[4 * LANES : CROWS, :] = halo
    xs[0] = xw_r[0:XP, :].astype(f32)
    xs[1] = xe_r[0:XP, :].astype(f32)
    south, north = edge_packs(xw_r, xe_r)
    low = lane_ids((8, LANES)) < 64
    for send, levels in ((up, (0, 1)), (down, (NL - 1, NL - 2))):
        for k, (kind, component, depth, column_at) in enumerate(FACE_ROWS):
            plane = PLANE_AT[(kind, component, levels[depth])]
            first, count = x_rows(plane)
            for c in range(4):
                for side in range(2):
                    at = c * XPLANE + first + (column_at if side == 0 else count - 1 - column_at)
                    to = c * 16 + side * 8 + k
                    rows_s[to : to + 1, :] = xs[side, at : at + 1, :]
            edge_col = jnp.where(low, unpack_north(north, plane), unpack_south(south, plane))
            for side in range(2):
                at = column_at if side == 0 else 7 - column_at
                to = 64 + side * 8 + k
                rows_s[to : to + 1, :] = edge_col[at : at + 1]
        send[CROWS:ZP, :] = rows_s[...].astype(bf16)
        pack, group = field_pack(ys_r), lane_ids((NX, LANES)) // 3
        moved = roll(field_pack(yn_r), 3 * APART, 1)
        for plane in sorted({PLANE_AT[(kind, component, levels[depth])] for kind, component, depth, _ in FACE_ROWS}):
            pack = jnp.where(group == plane + APART, moved, pack)
        send[ZP:ZROWS, :] = pack.astype(bf16)
    sort_pair("sec", down, up, ua, ub)


def flux_kernel(part, ua_r, ub_r, across_r, grid, ext, da, db, rows_s):
    got = [ref[4 * LANES : CROWS, :].astype(f32) for ref in (ua_r, ub_r, across_r)]
    turned = got[0] + got[1] + got[2]
    halo = jnp.concatenate([turned[0:8], jnp.zeros((LANES - 16, LANES), f32), turned[8:16]], axis=0).T
    for c in range(5):
        for f in range(4):
            at = c * LANES + f * NX
            total = part[at : at + NX, :]
            if c < 4:
                for ref in (ua_r, ub_r, across_r):
                    total = total + ref[at : at + NX, :].astype(f32)
            else:
                total = total + halo[f * NX : (f + 1) * NX]
            total = total * grid[MASK, c, OWN, :]
            ext[f, :, c * LANES : (c + 1) * LANES] = total
            rows_s[0, c * 16 + f * 4 : c * 16 + f * 4 + 4, :] = total[0:4]
            rows_s[1, c * 16 + f * 4 : c * 16 + f * 4 + 4, :] = total[NX - 4 : NX]
    first = jnp.where(even("gx"), 1, 0)
    da[...] = rows_s[first].astype(bf16)
    db[...] = rows_s[1 - first].astype(bf16)


def lane_next(value, lane):
    rolled = pltpu.roll(value, LANES - 1, 2)
    return jnp.where(lane == LANES - 1, jnp.concatenate([rolled[1:], rolled[:1]], axis=0), rolled)


def lane_prev(value, lane):
    rolled = pltpu.roll(value, 1, 2)
    return jnp.where(lane == 0, jnp.concatenate([rolled[-1:], rolled[:-1]], axis=0), rolled)


OWN, WEST, EAST = slice(12, 44), slice(8, 12), slice(44, 48)
PLANE = (5, 56, LANES)


MASK, BASE, VERT, KEPT = range(4)


def advance(here, above, below, velocity, grid, rows, open_below=None):
    r = rows.start
    lane = lane_ids((5, 8, LANES))

    def at(plane, c, where=rows):
        return plane[0][c, plane[1], :, where, :]

    base, vert, kept = (grid[k, :, rows, :] for k in (BASE, VERT, KEPT))
    if above is None:
        kept = kept + vert
    if open_below is not None:
        down = vert * open_below
        kept = kept + (vert - down)
    a, b = at(velocity, 0), at(velocity, 1)
    east, west, north, south = base - a, base + a, base - b, base + b
    results = []
    for c in range(2):
        g = at(here, c)
        new = kept * g
        new += east * at(here, c, slice(r + 1, r + 9)) + west * at(here, c, slice(r - 1, r + 7))
        new += north * lane_next(g, lane) + south * lane_prev(g, lane)
        if above is None:
            new += vert * at(below, c)
        elif open_below is None:
            new += vert * (at(above, c) + at(below, c))
        else:
            new += vert * at(above, c) + down * at(below, c)
        results.append(new)
    return results


def land_or(value, grid, rows, tr, c, level, x, out):
    for col in range(4):
        cells = slice(col * LANES, (col + 1) * LANES)
        out[:, cells] = jnp.where(grid[MASK, col, rows, :] > 0.0, value[col], tr[c, level, x : x + 8, cells])


def middle_kernel(
    tr, cu, yn_r, ys_r, xe_r, xw_r, table, after, after_zu, after_zd, g0, vel, g1, g2, grid, done, xs
):
    south, north = field_pack(yn_r), field_pack(ys_r)
    low = lane_ids((NX, LANES)) < 64
    edge_south, edge_north = edge_packs(xw_r, xe_r)
    edge_low = lane_ids((8, LANES)) < 64
    xs[0] = xw_r[0:XP, :].astype(f32)
    xs[1] = xe_r[0:XP, :].astype(f32)
    in_south, in_north, in_west, in_east = inside("gy", True), inside("gy", False), inside("gx", True), inside("gx", False)

    def pieces(plane, col, own):
        first, count = x_rows(plane)
        if col < 4:
            at = col * XPLANE + first
            east, west = xs[0, at : at + count, :], xs[1, at : at + count, :]
        else:
            own = jnp.where(low, unpack_north(north, plane), unpack_south(south, plane))
            edge = jnp.where(edge_low, unpack_north(edge_north, plane), unpack_south(edge_south, plane))
            east, west = edge[0:count], edge[8 - count : 8]
        return ((OWN, own), (slice(44, 44 + count), east), (slice(12 - count, 12), west))

    for col in range(5):
        own = None
        if col < 4:
            own = jnp.broadcast_to(column(table[LAND + col : LAND + col + 1, 0:NX]), (NX, LANES))
        for (rows, value), in_x in zip(pieces(MASK_PLANE, col, own), (1.0, in_east, in_west)):
            if col == 4:
                value = value * jnp.where(low[0 : value.shape[0]], in_north, in_south)
            grid[MASK, col, rows, :] = value * in_x
    lane = lane_ids((5, 8, LANES))
    for r in range(8, 48, 8):
        rows, m = slice(r, r + 8), grid[MASK, :, r : r + 8, :]
        around = grid[MASK, :, r + 1 : r + 9, :] + grid[MASK, :, r - 1 : r + 7, :] + lane_next(m, lane) + lane_prev(m, lane)
        grid[BASE, :, rows, :] = DIFFUSION * m
        grid[VERT, :, rows, :] = VERTICAL * m
        grid[KEPT, :, rows, :] = m * (1.0 - 2.0 * VERTICAL - DIFFUSION * around)

    for col in range(5):
        for plane, (kind, c, level) in enumerate(PLANES):
            source, target = (tr, g0) if kind == "t" else (cu, vel)
            own = source[c, level, :, col * LANES : (col + 1) * LANES] if col < 4 else None
            for rows, value in pieces(plane, col, own):
                scale = grid[MASK, col, rows, :]
                target[c, level, col, rows, :] = value * (scale if kind == "t" else ADVECTION * scale)

    def sweep(src, src_at, dst, dst_at, levels):
        def one_level(l, _):
            for r in range(8, 48, 8):
                rows = slice(r, r + 8)
                at = l - src_at
                step = advance((src, at), (src, at - 1), (src, at + 1), (vel, l - 3), grid, rows)
                for c, value in enumerate(step):
                    dst[c, l - dst_at, :, rows, :] = value
            return 0

        lax.fori_loop(levels[0], levels[1], one_level, 0, unroll=2)

    sweep(g0, 3, g1, 4, (4, 12))
    sweep(g1, 4, g2, 5, (5, 11))

    def last(l, _):
        for r in range(12, 44, 8):
            rows = slice(r, r + 8)
            at = l - 5
            step = advance((g2, at), (g2, at - 1), (g2, at + 1), (vel, l - 3), grid, rows)
            for c, value in enumerate(step):
                land_or(value, grid, rows, tr, c, l - 3, r - 12, done.at[c, l - 6, r - 12 : r - 4])
        return 0

    lax.fori_loop(6, 10, last, 0, unroll=2)


def face_steps(planes, velocities, levels, out, grid, tr, starts, last_starts, out_x=lambda x: x, open_below=None):
    for k in range(3):
        for l in levels[k]:
            here, above, below = (planes[k].get(i) for i in (l, l - 1, l + 1))
            floor = open_below if l == 12 else None
            for r in starts if k < 2 else last_starts:
                rows = slice(r, r + 8)
                step = advance(here, above, below, velocities[l], grid, rows, floor)
                for c, value in enumerate(step):
                    if k < 2:
                        ref, index = planes[k + 1][l]
                        ref[c, index, :, rows, :] = value
                    else:
                        x = r - 12
                        land_or(value, grid, rows, tr, c, l - 3, x, out.at[c, l - levels[2][0], out_x(x) : out_x(x) + 8])


def planes_of(*runs):
    return {first + k: (ref, index + k) for first, count, ref, index in runs for k in range(count)}


def forced(velocities, tracers):
    return (
        (velocities, 0, ADVECTION * WIND_GAIN),
        (velocities, 1, ADVECTION * WIND_GAIN),
        (tracers, 0, HEAT_GAIN),
        (tracers, 1, -SALT_GAIN),
    )


WHOLE, INNER = range(8, 48, 8), range(12, 44, 8)


def outer_kernel(
    tr, g0, vel, g1, g2, grid, zu_r, zd_r, ua_r, ub_r, ext, middle, after, out, ocean_flux, s0, sv, s1, s2,
    up_r, down_r, b0, bv, b1, b2, top, bottom, sems,
):
    sec = lax.axis_index("sec")
    writes = [
        pltpu.make_async_copy(ext.at[:, :, pl.ds(0, 512)], ocean_flux, sems.at[0]),
        pltpu.make_async_copy(middle.at[:, pl.ds(1, 3)], out.at[:, pl.ds(4, 3)], sems.at[1]),
        pltpu.make_async_copy(bottom, out.at[:, pl.ds(7, 3)], sems.at[2]),
    ]
    start(*writes[:2])
    sort_pair("sec", ua_r.at[pl.ds(CROWS, ZROWS - CROWS)], ub_r.at[pl.ds(CROWS, ZROWS - CROWS)], up_r, down_r)
    low = lane_ids((NX, LANES)) < 64

    def halo_planes(got, z, face, tracers, velocities):
        pack = got[ZP - CROWS : ZROWS - CROWS, :].astype(f32)
        near = [got[c * 16 : (c + 1) * 16, :].astype(f32) for c in range(5)]

        def put(target, body, plane, at, scale):
            for col in range(4):
                value = body[:, col * LANES : (col + 1) * LANES].astype(f32)
                target[col, OWN, :] = value * (scale * grid[MASK, col, OWN, :])
            if plane is None:
                return
            col4 = jnp.where(low, unpack_north(pack, plane), unpack_south(pack, plane + APART))
            target[4, OWN, :] = col4 * (scale * grid[MASK, 4, OWN, :])
            for col in range(5):
                for k, row in enumerate(at):
                    for to, value in ((44 + k, near[col][row : row + 1]), (11 - k, near[col][8 + row : 9 + row])):
                        target[col, to : to + 1, :] = value * (scale * grid[MASK, col, to : to + 1, :])

        for c in range(2):
            for k in range(3):
                depth = k if face == 1 else 2 - k
                level = k if face == 1 else 7 + k
                plane = PLANE_AT[("t", c, level)] if depth < 2 else None
                at = (3 * c, 3 * c + 1) if depth == 0 else (3 * c + 2,)
                put(tracers.at[c, k], z[c * 3 + k], plane, at, 1.0)
            for k in range(2):
                depth = k if face == 1 else 1 - k
                plane = PLANE_AT[("c", c, 0 if face == 1 else 9)] if depth == 0 else None
                put(velocities.at[c, k], z[6 + c * 2 + k], plane, (6 + c,), ADVECTION)

    halo_planes(up_r, zu_r, 1, b0, bv)
    face_steps(
        (
            planes_of((11, 2, g0, 8), (13, 3, b0, 0)),
            planes_of((10, 2, g1, 6), (12, 3, b1, 0)),
            planes_of((9, 2, g2, 4), (11, 3, b2, 0)),
        ),
        planes_of((10, 3, vel, 7), (13, 2, bv, 0)),
        (range(12, 15), range(11, 14), range(10, 13)),
        bottom, grid, tr, WHOLE, INNER,
        open_below=jnp.where(sec < lax.axis_size("sec") - 1, 1.0, 0.0).astype(f32),
    )
    writes[2].start()

    @pl.when(sec != 0)
    def _():
        level3 = pltpu.make_async_copy(middle.at[:, pl.ds(0, 1)], out.at[:, pl.ds(3, 1)], sems.at[3])
        level3.start()
        halo_planes(down_r, zd_r, 0, s0, sv)
        face_steps(
            (
                planes_of((0, 3, s0, 0), (3, 2, g0, 0)),
                planes_of((1, 3, s1, 0), (4, 2, g1, 0)),
                planes_of((2, 3, s2, 0), (5, 2, g2, 0)),
            ),
            planes_of((1, 2, sv, 0), (3, 3, vel, 0)),
            (range(1, 4), range(2, 5), range(3, 6)),
            top, grid, tr, WHOLE, INNER,
        )
        write = pltpu.make_async_copy(top.at[:, pl.ds(0, 3)], out.at[:, pl.ds(0, 3)], sems.at[4])
        write.start()
        wait(level3, write)

    @pl.when(sec == 0)
    def _():
        for f, (ref, c, gain) in enumerate(forced(sv, s0)):
            source = vel if f < 2 else g0
            for col in range(5):
                for r in range(8, 48, 8):
                    ref[c, 0, col, r : r + 8, :] = source[c, 0, col, r : r + 8, :]
                ref[c, 0, col, OWN, :] += gain * ext[f, :, col * LANES : (col + 1) * LANES] * grid[MASK, col, OWN, :]
        face_steps(
            surface_planes(s0, s1, s2, g0, g1, g2),
            planes_of((3, 1, sv, 0), (4, 3, vel, 1)),
            SURFACE_LEVELS,
            top, grid, tr, WHOLE, INNER,
        )
        write = pltpu.make_async_copy(top, out.at[:, pl.ds(0, 4)], sems.at[3])
        write.start()
        write.wait()

    wait(*writes)


SURFACE_LEVELS = (range(3, 5), range(3, 6), range(3, 7))


def surface_planes(s0, s1, s2, g0, g1, g2):
    return (
        planes_of((3, 1, s0, 0), (4, 2, g0, 1)),
        planes_of((3, 2, s1, 0), (5, 2, g1, 1)),
        planes_of((3, 3, s2, 0), (6, 2, g2, 1)),
    )


def surface_kernel(
    unfinished, tr, s0, sv, s1, s2, g0, vel, g1, g2, grid, db_r, da_r, out, e0, ev, e1, e2, edge, sems
):
    @pl.when(lax.axis_index("sec") == 0)
    def _():
        got_a, got_b = da_r[...].astype(f32), db_r[...].astype(f32)
        halo = (jnp.where(even("gx"), got_b, got_a), jnp.where(even("gx"), got_a, got_b))
        for c in range(2):
            for target, source, planes, groups in (
                (e0, s0, 1, (8, 16, 32, 40)),
                (ev, sv, 1, (8, 16, 32, 40)),
                (e1, s1, 2, (16, 32)),
                (e2, s2, 3, (16, 32)),
            ):
                for k in range(planes):
                    for r in groups:
                        target[c, k, :, r : r + 8, :] = source[c, k, :, r : r + 8, :]
        for side, rows in enumerate((WEST, EAST)):
            for f, (ref, c, gain) in enumerate(forced(ev, e0)):
                for col in range(5):
                    r = col * 16 + f * 4
                    ref[c, 0, col, rows, :] += gain * halo[side][r : r + 4] * grid[MASK, col, rows, :]
        face_steps(
            surface_planes(e0, e1, e2, g0, g1, g2),
            planes_of((3, 1, ev, 0), (4, 3, vel, 1)),
            SURFACE_LEVELS,
            edge, grid, tr, (8, 40), (12, 36), lambda x: 0 if x == 0 else 8,
        )
        writes = [
            pltpu.make_async_copy(
                edge.at[:, :, pl.ds(8 * side, 8)], out.at[:, pl.ds(0, 4), pl.ds(24 * side, 8)], sems.at[side]
            )
            for side in range(2)
        ]
        start(*writes)
        wait(*writes)


ANY = pl.BlockSpec(memory_space=pl.ANY)
HBM = pl.BlockSpec(memory_space=pltpu.HBM)
VMEM = pl.BlockSpec(memory_space=pltpu.VMEM)


def hbm(value):
    return pltpu.with_memory_space_constraint(value, pltpu.HBM)


def call(kernel, in_specs, outs, scratch, name, bytes_accessed, out_specs=None, aliases=None):
    return pl.pallas_call(
        kernel,
        out_shape=[jax.ShapeDtypeStruct(shape, dtype) for shape, dtype in outs],
        in_specs=in_specs,
        out_specs=out_specs or [VMEM] * len(outs),
        scratch_shapes=scratch,
        input_output_aliases=aliases or {},
        compiler_params=pltpu.CompilerParams(vmem_limit_bytes=VMEM_BYTES),
        cost_estimate=pl.CostEstimate(flops=0, bytes_accessed=bytes_accessed, transcendentals=0),
        name=name,
    )


def shifted(value, axis, step):
    count = lax.axis_size(axis)
    return lax.ppermute(value, axis, [(i, (i + step) % count) for i in range(count)])


def swapped(a, b, axis):
    count = lax.axis_size(axis)
    one = [(i, i ^ 1) for i in range(count)]
    other = [(i, (i + (1 if i % 2 else -1)) % count) for i in range(count)]
    b = lax.ppermute(b, axis, other)
    return lax.ppermute(a, axis, one), b


def on_device(air_surface, remap_weights, sources, live_count, land_sea, tracers, currents):
    src = hbm(jnp.transpose(sources[:, :, 0, :], (1, 2, 0)))
    live = hbm(jnp.transpose(live_count, (1, 2, 0)))
    land = hbm(jnp.transpose(land_sea, (1, 0)))
    dma = pltpu.SemaphoreType.DMA

    ya, yb, flux, table = call(
        pack_y_kernel,
        [HBM] * 7,
        [((YROWS, LANES), bf16), ((YROWS, LANES), bf16), ((NT, 4, NX, LANES), bf16), ((16, LANES), f32)],
        [
            pltpu.VMEM((YROWS, LANES), bf16),
            pltpu.VMEM((YROWS, LANES), bf16),
            pltpu.VMEM((NT, 2, NX), jnp.int32),
            pltpu.VMEM((NT, 1, NX), jnp.int32),
            pltpu.VMEM((NT, NX), jnp.int32),
            pltpu.VMEM((5, NX * NT, LANES), f32),
            pltpu.VMEM((NX, 2, 16, LANES), bf16),
            pltpu.VMEM((NX, 2, 16, LANES), bf16),
            pltpu.VMEM((192, LANES), f32),
            pltpu.VMEM((2, 2, 2, NL, NX, LANES), f32),
            dma((10,)),
        ],
        "pack_y",
        6_000_000,
    )(hbm(air_surface.reshape(5, NX * NT, LANES)), src, live, land, hbm(remap_weights), hbm(tracers), hbm(currents))
    ya_r, yb_r = swapped(ya, yb, "gy")

    zu, zd = call(
        pack_z_kernel,
        [ANY, ANY, ANY],
        [((10, NX, 512), bf16)] * 2,
        [pltpu.VMEM((2, 2, 3, NX, 512), f32), pltpu.VMEM((2, 2, 2, NX, 512), f32), dma((4,))],
        "pack_z",
        3_000_000,
    )(tracers, currents, table)
    zu_r = shifted(zu, "sec", -1)
    zd_r = shifted(zd, "sec", 1)

    xa, xb, yn_r, ys_r = call(
        pack_x_kernel,
        [VMEM, VMEM, VMEM, VMEM, ANY, ANY],
        [((XROWS, LANES), bf16)] * 2 + [((YROWS, LANES), bf16)] * 2,
        [pltpu.VMEM((XROWS, LANES), bf16)] * 2
        + [pltpu.VMEM((XP, LANES), f32), pltpu.VMEM((2, 2, 2, NL, 8, 512), f32), dma((4,))],
        "pack_x",
        3_000_000,
    )(flux, yb_r, ya_r, table, tracers, currents)
    xa_r, xb_r = swapped(xa, xb, "gx")

    first_part, wedge = call(
        remap_kernel,
        [VMEM] * 5 + [ANY],
        [((5 * LANES, LANES), f32), ((2, NT, 2, LANES, LANES), bf16)],
        [
            pltpu.VMEM((8, 4, 48, LANES), f32),
            pltpu.VMEM((2 * NT, 2 * LANES, LANES), f32),
        ],
        "remap",
        18_000_000,
    )(flux, yn_r, ys_r, table, remap_weights, xa)
    part, ua, ub, across, xe_r, xw_r = call(
        rim_kernel,
        [VMEM] * 7,
        [((5 * LANES, LANES), f32)]
        + [((rows, LANES), bf16) for rows in (ZROWS, ZROWS, CROWS, XROWS, XROWS)],
        [pltpu.VMEM((ZROWS, LANES), bf16)] * 2 + [pltpu.VMEM((2, XP, LANES), f32), pltpu.VMEM((80, LANES), f32)],
        "rim",
        4_000_000,
    )(first_part, wedge, yn_r, ys_r, xb_r, xa_r, table)
    across_r = shifted(across, "sec", 2)
    ua_r, ub_r = swapped(ua, ub, "sec")

    plane = (5, 56, LANES)
    g0, vel, g1, g2, grid, middle = call(
        middle_kernel,
        [VMEM] * 7 + [ANY] * 3,
        [
            ((2, NL) + plane, f32),
            ((2, NL) + plane, f32),
            ((2, NL - 2) + plane, f32),
            ((2, NL - 4) + plane, f32),
            ((4,) + plane, f32),
            ((2, NL - 6, NX, 512), f32),
        ],
        [
            pltpu.VMEM((2, XP, LANES), f32),
        ],
        "middle",
        20_000_000,
    )(tracers, currents, yn_r, ys_r, xe_r, xw_r, table, across, zu_r, zd_r)

    ext, da, db = call(
        flux_kernel,
        [VMEM] * 5,
        [((4, NX, 5 * LANES), f32), ((80, LANES), bf16), ((80, LANES), bf16)],
        [pltpu.VMEM((2, 80, LANES), f32)],
        "flux_sum",
        3_000_000,
    )(part, ua_r, ub_r, across_r, grid)
    da_r, db_r = swapped(da, db, "gx")

    unfinished, ocean_flux, s0, sv, s1, s2 = call(
        outer_kernel,
        [VMEM] * 12 + [ANY],
        [((2, NL, NX, 512), f32), ((4, NX, 512), f32)] + [((2, count) + plane, f32) for count in (3, 2, 3, 3)],
        [pltpu.VMEM((ZROWS - CROWS, LANES), bf16)] * 2
        + [pltpu.VMEM((2, count) + plane, f32) for count in (3, 2, 3, 3)]
        + [pltpu.VMEM((2, 4, NX, 512), f32), pltpu.VMEM((2, 3, NX, 512), f32), dma((5,))],
        "outer",
        18_000_000,
        [HBM, HBM] + [VMEM] * 4,
    )(tracers, g0, vel, g1, g2, grid, zu_r, zd_r, ua_r, ub_r, ext, middle, da)

    (tracers_out,) = call(
        surface_kernel,
        [HBM] + [VMEM] * 12,
        [((2, NL, NX, 512), f32)],
        [pltpu.VMEM((2, count) + plane, f32) for count in (1, 1, 2, 3)]
        + [pltpu.VMEM((2, 4, 16, 512), f32), dma((2,))],
        "surface",
        8_000_000,
        [HBM],
        {0: 0},
    )(unfinished, tracers, s0, sv, s1, s2, g0, vel, g1, g2, grid, db_r, da_r)
    return (tracers_out, ocean_flux)


def solution(mesh):
    return jax.shard_map(
        on_device,
        mesh=mesh,
        in_specs=(
            P(None, "gx", "gy", "sec", None),
            P("gx", "gy", "sec", None, None, None),
            P("gx", "gy", "sec", None),
            P("gx", "gy", "sec"),
            P("gx", "gy"),
            P(None, "sec", "gx", "gy"),
            P(None, "sec", "gx", "gy"),
        ),
        out_specs=(P(None, "sec", "gx", "gy"), P(None, "gx", "gy")),
        check_vma=False,
    )
```
